256 devices in a mesh: dp: 4 (over x_lo, core), fsdp: 64 (over z, y, x_hi).
Axes of the slice: x: 4 (x_hi: 2, x_lo: 2; x = x_hi * 2 + x_lo), y: 4, z: 8, core: 2. Of those that a mesh axis runs over, the one named last changes fastest.
Arguments:
- tokens: bfloat16 [98304, 5120], P(('dp', 'fsdp')), may hold values from -50 to 50
- codes: bfloat16 [5120, 1024], P('fsdp'), may hold values from -0.078125 to 0.078125
- scales: float32 [5120, 8], P('fsdp'), may hold values from 0.5 to 2
- norm_gain: float32 [1024], replicated, may hold values from 0.25 to 1.75
- key_grad: bfloat16 [98304, 1024], P(('dp', 'fsdp')), may hold values from -120 to 120
Outputs:
- keys: bfloat16 [98304, 1024], P(('dp', 'fsdp'))
- token_grad: bfloat16 [98304, 5120], P(('dp', 'fsdp'))
- weight_grad: float32 [5120, 1024], P('fsdp')
- gain_grad: float32 [1024], replicated
The draws below stay inside these ranges and needn't reach their ends.
All inputs are finite; a program needn't handle non-finite values.
Results may differ from the reference program's by a relative error of at most 0.015.
Values may be sent and summed in bfloat16 or wider, within the bound.
A program may use at most 192 MiB of HBM per device.

```python
import math
import jax
import jax.numpy as jnp
from jax import lax

D = 5120
BLOCK = 128
TOK_DEV = 384
W = 1024
TOKENS = 98304


def draw_tokens(key, part):
    key = jax.random.fold_in(key, 11)
    first, second = jax.random.split(key, 2)
    row_scale = jnp.exp(jax.random.uniform(first, (TOKENS, 1), jnp.float32) * math.log(10.0))
    values = row_scale * jnp.clip(jax.random.normal(second, (TOKENS, D), jnp.float32), -4.0, 4.0)
    return values.astype(jnp.bfloat16)


def draw_key_grad(key, part):
    key = jax.random.fold_in(key, 23)
    first, second = jax.random.split(key, 2)
    row_scale = jnp.exp(jax.random.uniform(first, (TOKENS, 1), jnp.float32) * math.log(10.0))
    rising = 1.0 + 2.0 * jnp.arange(TOKENS, dtype=jnp.float32)[:, None] / max(TOKENS - 1, 1)
    values = rising * row_scale * jnp.clip(jax.random.normal(second, (TOKENS, W), jnp.float32), -4.0, 4.0)
    return values.astype(jnp.bfloat16)


def steps_of(rng, dims, pieces, low, high):
    loudness = 1.0
    for axis_at, shards_of in pieces:
        heights = jax.random.uniform(jax.random.fold_in(jax.random.fold_in(rng, 6), axis_at), (shards_of,), jnp.float32, low / len(pieces), high / len(pieces))
        loudness = loudness * jnp.repeat(jnp.exp(heights), dims[axis_at] // shards_of).reshape((-1,) + (1,) * (len(dims) - 1 - axis_at))
    return loudness


def normal_values(key, extent, width, reach, pieces=(), kind=jnp.bfloat16):
    array = jax.random.normal(key, extent, jnp.float32) * width
    if len(pieces) > 0:
        array = steps_of(key, extent, pieces, -0.22, 0.18) * array
    return jnp.clip(array, min=-reach, max=reach).astype(kind)


def setup_inputs(seed: int = 0) -> dict:
    seeds = jax.random.split(jax.random.key(seed), 6)
    return {
        "tokens": draw_tokens(jax.random.fold_in(seeds[5], 71), 0),
        "codes": normal_values(seeds[1], (D, W), D ** -0.5, 0.078125, ((0, 64),)),
        "scales": jnp.clip(jnp.exp(math.log(2.0) - 1.3862944 * jax.random.uniform(seeds[2], (D, W // BLOCK), jnp.float32) ** steps_of(seeds[2], (D, W // BLOCK), ((0, 64),), -0.2, 0.2)), 0.5, 2.0),
        "norm_gain": jnp.clip(1.0 + 0.15 * jax.random.normal(seeds[3], (W,), jnp.float32), 0.25, 1.75),
        "key_grad": draw_key_grad(jax.random.fold_in(seeds[5], 71), 0),
    }


eps = 1e-06

def reference(tokens, codes, scales, norm_gain, key_grad):
    weight = (codes.astype(jnp.float32) * jnp.repeat(scales, BLOCK, axis=1)).astype(jnp.bfloat16)
    k_raw = jnp.dot(tokens, weight, preferred_element_type=jnp.float32)
    rinv = lax.rsqrt(lax.optimization_barrier(jnp.mean(k_raw * k_raw, axis=1, keepdims=True)) + eps)
    normed = k_raw * rinv
    keys = (normed * norm_gain).astype(jnp.bfloat16)
    grads = key_grad.astype(jnp.float32)
    gain_grad = lax.optimization_barrier(jnp.sum(grads * normed, axis=0))
    dnorm = grads * norm_gain
    d_raw = (rinv * (dnorm - normed * lax.optimization_barrier(jnp.mean(dnorm * normed, axis=1, keepdims=True)))).astype(jnp.bfloat16)
    token_grad = lax.dot_general(d_raw, weight, (((1,), (1,)), ((), ())), preferred_element_type=jnp.float32).astype(jnp.bfloat16)
    blocks = TOKENS // TOK_DEV
    tok_blocks = tokens.reshape(blocks, TOK_DEV, D)
    grad_blocks = d_raw.reshape(blocks, TOK_DEV, W)

    def accumulate(total, pair):
        partial_value = lax.dot_general(pair[0], pair[1], (((0,), (0,)), ((), ())), preferred_element_type=jnp.float32)
        rounded = lax.optimization_barrier(partial_value.astype(jnp.bfloat16))
        return (total + rounded.astype(jnp.float32), None)
    weight_grad, unused = lax.scan(accumulate, jnp.zeros((D, W), jnp.float32), (tok_blocks, grad_blocks))
    return (keys, token_grad, weight_grad, gain_grad)
```

```python
import jax
import jax.numpy as jnp
from jax import lax
from jax.experimental import pallas as pl
from jax.experimental.pallas import tpu as pltpu
from jax.sharding import PartitionSpec as P

MESH = pl.DeviceIdType.MESH
F32, BF16 = jnp.float32, jnp.bfloat16
BLOCK = 128
EPS = 1e-06
D, W, T, ROWS = 5120, 1024, 384, 80
HALF = W // 2
SLAB = 640
PAIR = 2 * SLAB
RA, RB, RC = 96, 96, 128
HA, HB, HC = RA // 2, RB // 2, RC // 2
OFF_A, OFF_B, OFF_C = 0, RA - ROWS, RA + RB - 2 * ROWS
NX, NY, NZ = 4, 4, 8


def segments(rows, block, offset, half):
    cuts = []
    for first, last, row, column in ((0, ROWS, 0, block), (ROWS, rows, offset, 3)):
        if first < half < last:
            cuts += [(first, half, row, column), (half, last, row + half - first, column)]
        else:
            cuts.append((first, last, row, column))
    return cuts


SEG_A = segments(RA, 0, OFF_A, HA)
SEG_B = segments(RB, 1, OFF_B, HB)
SEG_C = segments(RC, 2, OFF_C, HC)


def column(block):
    return pl.ds(block * BLOCK, BLOCK)


def rem(a, n):
    return lax.rem(a + 2 * n, n)


def add(*refs):
    total = refs[0][...].astype(F32)
    for ref in refs[1:]:
        total = total + ref[...].astype(F32)
    return total


def kernel(
    tokens, codes, scales, gain, key_grad,
    keys_out, tg_out, wg_out, gg_out,
    tokv, tokt, kgv, wf, wa, wb, wc, acc, draw, keyv, stats,
    ga, gb, gc, raf, ran, rb, rc, ray, rax, rbx, rbz, rcy, rcz, tgr, gsend, grecv, gfin, fin, stage,
    s_loc, s_out,
    s_d2d, r_d2d, s_ax, r_ax, s_ay, r_ay, s_az, r_az, s_z, r_z, s_bx, r_bx, s_cy, r_cy, s_ring, r_ring,
    s_raf, r_raf, s_ran, r_ran, s_rr, r_rr, s_one, r_one, s_gain, r_gain, s_fin, r_fin,
):
    dp, fs = lax.axis_index("dp"), lax.axis_index("fsdp")
    xl, core = dp // 2, lax.rem(dp, 2)
    z, y, xh = fs // 8, lax.rem(fs // 2, 4), lax.rem(fs, 2)
    x = xh * 2 + xl
    other = 1 - core
    sign = 2 * lax.rem(z, 2) - 1

    def dev(x_, y_, z_, c_):
        x_, y_, z_ = rem(x_, NX), rem(y_, NY), rem(z_, NZ)
        return (lax.rem(x_, 2) * 2 + c_, z_ * 8 + y_ * 2 + x_ // 2)

    def copy(src, dst, send, recv, device):
        return pltpu.make_async_remote_copy(
            src_ref=src, dst_ref=dst, send_sem=send, recv_sem=recv, device_id=device, device_id_type=MESH
        )

    def pair(k):
        return rem(z // 2 + sign * (k + k // 2 - 2 * (k // 3)), 4)

    def loop(n, body, first=0):
        lax.fori_loop(first, n, lambda i, c: (body(i), c)[1], 0)

    sib = dev(x, y, z, other)

    def c_tok(p):
        cols = pl.ds(p * PAIR, PAIR)
        return pltpu.make_async_copy(tokens.at[:, cols], tokv.at[pl.ds(core * T, T), cols], s_loc.at[p])

    def d_tok(p):
        cols = pl.ds(p * PAIR, PAIR)
        return copy(tokens.at[:, cols], tokv.at[pl.ds(core * T, T), cols], s_d2d.at[p], r_d2d.at[p], sib)

    def c_kg():
        return pltpu.make_async_copy(
            key_grad.at[:, pl.ds(core * HALF, HALF)], kgv.at[pl.ds(core * T, T)], s_loc.at[4]
        )

    def d_kg():
        return copy(
            key_grad.at[:, pl.ds(other * HALF, HALF)], kgv.at[pl.ds(core * T, T)], s_d2d.at[4], r_d2d.at[4], sib
        )

    def d_stats():
        return copy(stats.at[0], stats.at[1], s_d2d.at[5], r_d2d.at[5], sib)

    def d_keys():
        return copy(
            keyv.at[pl.ds(other * T, T)], keys_out.at[:, pl.ds(core * HALF, HALF)], s_d2d.at[6], r_d2d.at[6], sib
        )

    def c_keys():
        return pltpu.make_async_copy(
            keyv.at[pl.ds(core * T, T)], keys_out.at[:, pl.ds(core * HALF, HALF)], s_out.at[4]
        )

    def d_tg(p):
        cols = pl.ds(p * PAIR, PAIR)
        return copy(tokv.at[pl.ds(other * T, T), cols], tgr.at[:, cols], s_d2d.at[7 + p], r_d2d.at[7 + p], sib)

    def c_tg(p):
        cols = pl.ds(p * PAIR, PAIR)
        return pltpu.make_async_copy(tokv.at[pl.ds(core * T, T), cols], tg_out.at[:, cols], s_out.at[p])

    def m_ax():
        ref = wa.at[z, y, xh]
        return copy(ref, ref, s_ax.at[0], r_ax.at[0], dev(3 - x, y, z, core))

    def m_ay(j):
        ref = wa.at[z, y]
        return copy(ref, ref, s_ay.at[j - 1], r_ay.at[j - 1], dev(x, y + j, z, core))

    def m_az(d, s, h):
        sg = 1 - 2 * d
        ref = wa.at[rem(z - sg * s, NZ), pl.ds(2 * h, 2)]
        at = (s * 2 + h) * 2 + d
        return copy(ref, ref, s_az.at[at], r_az.at[at], dev(x, y, z + sg, core))

    def m_bz(j):
        ref = wb.at[y, z, xh, xl]
        return copy(ref, ref, s_z.at[j - 1], r_z.at[j - 1], dev(x, y, z + j, core))

    def m_cz(j):
        ref = wc.at[x, z, y]
        return copy(ref, ref, s_z.at[6 + j], r_z.at[6 + j], dev(x, y, z + j, core))

    def m_bx(k, j):
        ref = wb.at[y, pl.ds(2 * pair(k), 2), xh, xl]
        return copy(ref, ref, s_bx.at[k * 3 + j - 1], r_bx.at[k * 3 + j - 1], dev(x + j, y, z, core))

    def m_cy(k, j):
        ref = wc.at[x, pl.ds(2 * pair(k), 2), y]
        return copy(ref, ref, s_cy.at[k * 3 + j - 1], r_cy.at[k * 3 + j - 1], dev(x, y + j, z, core))

    def m_by(k, d, hop):
        sg = 1 - 2 * d
        if hop == 0:
            ref = wb.at[y, pl.ds(2 * pair(k), 2)]
        else:
            ref = wb.at[rem(y - sg, NY), 2 * pair(k) + d]
        at = (k * 2 + hop) * 2 + d
        return copy(ref, ref, s_ring.at[at], r_ring.at[at], dev(x, y + sg, z, core))

    def m_cx(k, d, hop):
        sg = 1 - 2 * d
        if hop == 0:
            ref = wc.at[x, pl.ds(2 * pair(k), 2)]
        else:
            ref = wc.at[rem(x - sg, NX), 2 * pair(k) + d]
        at = 16 + (k * 2 + hop) * 2 + d
        return copy(ref, ref, s_ring.at[at], r_ring.at[at], dev(x + sg, y, z, core))

    def m_f(d, s, first=False):
        sg = 1 - 2 * d
        src = ga.at[rem(z + 4, NZ), pl.ds(2 * d, 2)] if first else raf.at[d, s - 1]
        return copy(src, raf.at[d, s], s_raf.at[d * 4 + s], r_raf.at[d * 4 + s], dev(x, y, z + sg, core))

    def m_n(d, s, first=False):
        sg = 1 - 2 * d
        src = ga.at[rem(z + 3 * sg, NZ), pl.ds(2 * (1 - d), 2)] if first else ran.at[d, s - 2]
        return copy(src, ran.at[d, s - 1], s_ran.at[d * 3 + s - 1], r_ran.at[d * 3 + s - 1], dev(x, y, z + sg, core))

    def m_rb(k, d, what):
        sg = 1 - 2 * d
        q = pair(3 - k)
        src = (
            gb.at[rem(y + 2, NY), 2 * q + d],
            gb.at[rem(y + sg, NY), 2 * q + 1 - d],
            rb.at[k, d, 0],
        )[what]
        at = (k * 2 + d) * 3 + what
        return copy(src, rb.at[k, d, what], s_rr.at[at], r_rr.at[at], dev(x, y + sg, z, core))

    def m_rc(k, d, what):
        sg = 1 - 2 * d
        q = pair(3 - k)
        src = (
            gc.at[rem(x + 2, NX), 2 * q + d],
            gc.at[rem(x + sg, NX), 2 * q + 1 - d],
            rc.at[k, d, 0],
        )[what]
        at = 24 + (k * 2 + d) * 3 + what
        return copy(src, rc.at[k, d, what], s_rr.at[at], r_rr.at[at], dev(x + sg, y, z, core))

    def m_rbx(k, j):
        to = rem(x + j, NX)
        zs = pl.ds(2 * pair(3 - k), 2)
        at = k * 3 + j - 1
        return copy(
            gb.at[y, zs, to // 2, lax.rem(to, 2)], rbx.at[j - 1, zs], s_one.at[at], r_one.at[at], dev(to, y, z, core)
        )

    def m_rcy(k, j):
        to = rem(y + j, NY)
        zs = pl.ds(2 * pair(3 - k), 2)
        at = 12 + k * 3 + j - 1
        return copy(gc.at[x, zs, to], rcy.at[j - 1, zs], s_one.at[at], r_one.at[at], dev(x, to, z, core))

    def m_rbz(j):
        to = rem(z + j, NZ)
        at = 23 + j
        return copy(gb.at[y, to, xh, xl], rbz.at[j - 1], s_one.at[at], r_one.at[at], dev(x, y, to, core))

    def m_rcz(j):
        to = rem(z + j, NZ)
        at = 30 + j
        return copy(gc.at[x, to, y], rcz.at[j - 1], s_one.at[at], r_one.at[at], dev(x, y, to, core))

    def m_ray(j):
        to = rem(y + j, NY)
        at = 37 + j
        return copy(ga.at[z, to], ray.at[j - 1], s_one.at[at], r_one.at[at], dev(x, to, z, core))

    def m_rax(j):
        to = rem(x + j, NX)
        at = 40 + j
        src = ga.at[z, y, to // 2, pl.ds(lax.rem(to, 2) * HA, HA)]
        return copy(src, rax.at[j - 1], s_one.at[at], r_one.at[at], dev(to, y, z, core))

    def m_gx(j):
        return copy(gsend.at[0], grecv.at[j - 1], s_gain.at[j - 1], r_gain.at[j - 1], dev(x + j, y, z, core))

    def m_gy(j):
        return copy(gsend.at[1], grecv.at[2 + j], s_gain.at[2 + j], r_gain.at[2 + j], dev(x, y + j, z, core))

    def m_gz(j):
        return copy(gsend.at[2], grecv.at[5 + j], s_gain.at[5 + j], r_gain.at[5 + j], dev(x, y, z + j, core))

    def m_gs():
        return copy(gfin.at[core], gfin.at[core], s_gain.at[13], r_gain.at[13], sib)

    partner = x + 1 - 2 * xl
    fins = (dev(partner, y, z, core), sib, dev(partner, y, z, other))

    def m_fin(i):
        return copy(fin.at[xl, core], fin.at[xl, core], s_fin.at[i], r_fin.at[i], fins[i])

    loop(4, lambda p: c_tok(p).start())
    c_kg().start()

    barrier = pltpu.get_barrier_semaphore()

    def signal(device):
        pl.semaphore_signal(barrier, inc=1, device_id=device, device_id_type=MESH)

    loop(NX, lambda j: signal(dev(x + j, y, z, core)), 1)
    loop(NY, lambda j: signal(dev(x, y + j, z, core)), 1)
    loop(NZ, lambda j: signal(dev(x, y, z + j, core)), 1)
    signal(sib)
    signal(fins[2])

    for b in range(4):
        scale = jnp.where(core == 0, scales[:, b : b + 1], scales[:, 4 + b : 5 + b])
        code = codes[:, pl.ds(pl.multiple_of(core * HALF + b * BLOCK, BLOCK), BLOCK)]
        stage[:, column(b)] = (code.astype(F32) * scale).astype(BF16)
    for first, last, row, block in SEG_A:
        wa[z, y, xh, first:last] = stage[row : row + last - first, column(block)]
    for mine in range(2):

        @pl.when(xl == mine)
        def _():
            for first, last, row, block in SEG_B:
                if first // HB == mine:
                    wb[y, z, xh, mine, first - mine * HB : last - mine * HB] = stage[row : row + last - first, column(block)]
            for first, last, row, block in SEG_C:
                if first // HC == mine:
                    wc[x, z, y, first - mine * HC : last - mine * HC] = stage[row : row + last - first, column(block)]

    pl.semaphore_wait(barrier, 15)
    m_ax().start()
    loop(NZ, lambda j: m_cz(j).start(), 1)
    loop(NZ, lambda j: m_bz(j).start(), 1)
    d_kg().start()
    loop(4, lambda k: d_tok(pair(k)).start())

    m_ax().wait_recv()
    loop(NY, lambda j: m_ay(j).start(), 1)
    loop(NZ, lambda j: m_cz(j).wait_recv(), 1)
    loop(4, lambda k: loop(NY, lambda j: m_cy(k, j).start(), 1))
    loop(NY, lambda j: m_ay(j).wait_recv(), 1)
    for d in range(2):
        m_az(d, 0, d).start()
    for d in range(2):
        m_az(d, 0, 1 - d).start()
    loop(NZ, lambda j: m_bz(j).wait_recv(), 1)
    loop(4, lambda k: loop(NX, lambda j: m_bx(k, j).start(), 1))

    def own_rings(k):
        loop(NY, lambda j: m_cy(k, j).wait_recv(), 1)
        for d in range(2):
            m_cx(k, d, 0).start()
        loop(NX, lambda j: m_bx(k, j).wait_recv(), 1)
        for d in range(2):
            m_by(k, d, 0).start()

    loop(4, own_rings)
    acc[...] = jnp.zeros_like(acc)
    loop(4, lambda p: c_tok(p).wait())
    c_kg().wait()
    d_kg().wait_recv()

    def consume(k):
        for d in range(2):
            m_cx(k, d, 1).wait_recv()
            m_by(k, d, 1).wait_recv()
        p = pair(k)

        def rows_of(i):
            zz, yy, hh = 2 * p + i // 8, lax.rem(i // 2, 4), lax.rem(i, 2)
            base = zz * SLAB + yy * 160 + hh * ROWS
            for first, last, row, block in SEG_A:
                wf[pl.ds(pl.multiple_of(base + row, 16), last - first), column(block)] = wa[zz, yy, hh, first:last]
            for first, last, row, block in SEG_B:
                at = first // HB
                wf[pl.ds(pl.multiple_of(base + row, 16), last - first), column(block)] = wb[
                    yy, zz, hh, at, first - at * HB : last - at * HB
                ]
            for first, last, row, block in SEG_C:
                at = first // HC
                wf[pl.ds(pl.multiple_of(base + row, 16), last - first), column(block)] = wc[
                    2 * hh + at, zz, yy, first - at * HC : last - at * HC
                ]

        loop(16, rows_of)
        begin = pl.multiple_of(p * PAIR, BLOCK)
        acc[...] += jnp.dot(tokv[:, pl.ds(begin, PAIR)], wf[pl.ds(begin, PAIR), :], preferred_element_type=F32)

    def transpose(k):
        d_tok(pair(k)).wait_recv()

        def part(i):
            begin = pl.multiple_of(pair(k) * PAIR + i * 256, BLOCK)
            tokt[pl.ds(begin, 256), :] = tokv[:, pl.ds(begin, 256)].T

        loop(5, part)

    def ring(k):
        transpose(k)
        for d in range(2):
            m_cx(k, d, 0).wait_recv()
            m_cx(k, d, 1).start()
            m_by(k, d, 0).wait_recv()
            m_by(k, d, 1).start()
        for d in range(2):
            m_az(d, k, d).wait_recv()

            @pl.when(k < 3)
            def _():
                m_az(d, k + 1, d).start()

        @pl.when(k < 3)
        def _():
            for d in range(2):
                m_az(d, k, 1 - d).wait_recv()

                @pl.when(k < 2)
                def _():
                    m_az(d, k + 1, 1 - d).start()

        @pl.when(k > 0)
        def _():
            consume(k - 1)

    loop(4, ring)
    consume(3)

    gains = gain[0:1, pl.ds(pl.multiple_of(core * HALF, BLOCK), HALF)]
    lane = lax.broadcasted_iota(jnp.int32, (8, BLOCK), 1)
    CH = 64
    stats[0] = jnp.zeros((2, 8, BLOCK), F32)

    def sums(i):
        rows = pl.ds(pl.multiple_of(i * CH, CH), CH)
        k_raw = acc[rows, :]
        dn = kgv[rows, :].astype(F32) * gains
        one = jnp.sum(k_raw * k_raw, axis=1, keepdims=True)
        two = jnp.sum(dn * k_raw, axis=1, keepdims=True)
        for j in range(CH // 8):
            here = lane == i * (CH // 8) + j
            stats[0, 0] = jnp.where(here, one[8 * j : 8 * j + 8], stats[0, 0])
            stats[0, 1] = jnp.where(here, two[8 * j : 8 * j + 8], stats[0, 1])

    loop(2 * T // CH, sums)
    d_stats().start()
    d_stats().wait_recv()
    stats[2] = (stats[0] + stats[1]) * (1.0 / W)
    gsend[0] = jnp.zeros((8, HALF), F32)

    def factors(i):
        rinvs, means = [], []
        for j in range(CH // 8):
            here = lane == i * (CH // 8) + j
            rinv = lax.rsqrt(jnp.sum(jnp.where(here, stats[2, 0], 0.0), axis=1, keepdims=True) + EPS)
            rinvs.append(rinv)
            means.append(rinv * jnp.sum(jnp.where(here, stats[2, 1], 0.0), axis=1, keepdims=True))
        return jnp.concatenate(rinvs, axis=0), jnp.concatenate(means, axis=0)

    def norm(i):
        rows = pl.ds(pl.multiple_of(i * CH, CH), CH)
        rinv, mean = factors(i)
        normed = acc[rows, :] * rinv
        grads = kgv[rows, :].astype(F32)
        draw[rows, :] = (rinv * (grads * gains - normed * mean)).astype(BF16)
        keyv[rows, :] = (normed * gains).astype(BF16)
        gsend[0] += jnp.sum((grads * normed).reshape(CH // 8, 8, HALF), axis=0)

    loop(2 * T // CH, norm)

    def grad(k):
        q = pair(3 - k)

        def slab(i):
            zz = 2 * q + i
            begin = pl.multiple_of(zz * SLAB, BLOCK)
            part = jnp.dot(tokt[pl.ds(begin, SLAB), :], draw[...], preferred_element_type=F32).astype(BF16)
            for yy in range(NY):
                for hh in range(2):
                    base = yy * 160 + hh * ROWS
                    for first, last, row, block in SEG_A:
                        value = part[base + row : base + row + last - first, block * BLOCK : (block + 1) * BLOCK]
                        ga[zz, yy, hh, first:last] = value
                    for first, last, row, block in SEG_B:
                        value = part[base + row : base + row + last - first, block * BLOCK : (block + 1) * BLOCK]
                        at = first // HB
                        gb[yy, zz, hh, at, first - at * HB : last - at * HB] = value
                    for first, last, row, block in SEG_C:
                        value = part[base + row : base + row + last - first, block * BLOCK : (block + 1) * BLOCK]
                        at = first // HC
                        gc[2 * hh + at, zz, yy, first - at * HC : last - at * HC] = value

        loop(2, slab)
        for d in range(2):
            m_rc(k, d, 0).start()
            m_rb(k, d, 0).start()

        @pl.when(k == 0)
        def _():
            for d in range(2):
                m_f(d, 0, True).start()

        @pl.when(k == 1)
        def _():
            for d in range(2):
                m_n(d, 1, True).start()

        for d in range(2):
            m_rc(k, d, 1).start()
            m_rb(k, d, 1).start()

    loop(4, grad)
    d_keys().start()
    c_keys().start()
    loop(NX, lambda j: m_gx(j).start(), 1)

    def finish(k):
        q = pair(3 - k)
        for d in range(2):
            m_rc(k, d, 1).wait_recv()
            m_rc(k, d, 2).wait_recv()
        for h in range(2):
            ref = gc.at[x, 2 * q + h]
            ref[...] = add(ref, rc.at[k, h, 2], rc.at[k, 1 - h, 1]).astype(BF16)
        loop(NY, lambda j: m_rcy(k, j).start(), 1)
        for d in range(2):
            m_rb(k, d, 1).wait_recv()
            m_rb(k, d, 2).wait_recv()
        for h in range(2):
            ref = gb.at[y, 2 * q + h]
            ref[...] = add(ref, rb.at[k, h, 2], rb.at[k, 1 - h, 1]).astype(BF16)
        loop(NX, lambda j: m_rbx(k, j).start(), 1)

    def token_part(p):
        begin = pl.multiple_of(p * PAIR, BLOCK)
        weight = wf[pl.ds(begin, PAIR), :]
        for to in (other, core):
            rows = pl.ds(pl.multiple_of(to * T, T), T)
            tokv[rows, pl.ds(begin, PAIR)] = lax.dot_general(
                draw[rows, :], weight, (((1,), (1,)), ((), ())), preferred_element_type=F32
            ).astype(BF16)
        d_tg(p).start()

    def reduce(k):
        for d in range(2):
            sg = 1 - 2 * d
            q = pair(3 - k)
            m_rc(k, d, 0).wait_recv()
            ref = rc.at[k, d, 0]
            ref[...] = add(ref, gc.at[rem(x + sg, NX), 2 * q + d]).astype(BF16)
            m_rc(k, d, 2).start()
            m_rb(k, d, 0).wait_recv()
            ref = rb.at[k, d, 0]
            ref[...] = add(ref, gb.at[rem(y + sg, NY), 2 * q + d]).astype(BF16)
            m_rb(k, d, 2).start()

        @pl.when(k < 3)
        def _():
            for d in range(2):
                sg = 1 - 2 * d
                m_f(d, k, True).wait_recv()
                ref = raf.at[d, k]
                ref[...] = add(ref, ga.at[rem(z + sg * (3 - k), NZ), pl.ds(2 * d, 2)]).astype(BF16)
                m_f(d, k + 1).start()

            @pl.when(k > 0)
            def _():
                for d in range(2):
                    sg = 1 - 2 * d
                    m_n(d, k, True).wait_recv()
                    ref = ran.at[d, k - 1]
                    ref[...] = add(ref, ga.at[rem(z + sg * (3 - k), NZ), pl.ds(2 * (1 - d), 2)]).astype(BF16)
                    m_n(d, k + 1).start()

        token_part(k)

        @pl.when(k > 0)
        def _():
            finish(k - 1)

    loop(4, reduce)
    loop(NX, lambda j: m_gx(j).wait_recv(), 1)
    gsend[1] = add(gsend.at[0], *(grecv.at[i] for i in range(3)))
    loop(NY, lambda j: m_gy(j).start(), 1)
    for d in range(2):
        m_f(d, 3, True).wait_recv()
        m_n(d, 3, True).wait_recv()
    for h in range(2):
        ref = ga.at[z, pl.ds(2 * h, 2)]
        ref[...] = add(ref, raf.at[h, 3], ran.at[1 - h, 2]).astype(BF16)
    loop(NY, lambda j: m_ray(j).start(), 1)
    finish(3)

    loop(NY, lambda j: m_ray(j).wait_recv(), 1)
    ref = ga.at[z, y]
    ref[...] = add(ref, *(ray.at[i] for i in range(3))).astype(BF16)
    loop(NX, lambda j: m_rax(j).start(), 1)
    loop(NY, lambda j: m_gy(j).wait_recv(), 1)
    gsend[2] = add(gsend.at[1], *(grecv.at[3 + i] for i in range(3)))
    loop(NZ, lambda j: m_gz(j).start(), 1)

    loop(4, lambda k: loop(NY, lambda j: m_rcy(k, j).wait_recv(), 1))

    def sum_c(zz):
        ref = gc.at[x, zz, y]
        ref[...] = add(ref, *(rcy.at[i, zz] for i in range(3))).astype(BF16)

    loop(NZ, sum_c)
    loop(NZ, lambda j: m_rcz(j).start(), 1)
    loop(4, lambda k: loop(NX, lambda j: m_rbx(k, j).wait_recv(), 1))

    def sum_b(zz):
        ref = gb.at[y, zz, xh, xl]
        ref[...] = add(ref, *(rbx.at[i, zz] for i in range(3))).astype(BF16)

    loop(NZ, sum_b)
    loop(NZ, lambda j: m_rbz(j).start(), 1)

    def token_sum(p):
        d_tg(p).wait()
        begin = pl.multiple_of(p * PAIR, BLOCK)
        cols = pl.ds(begin, PAIR)
        rows = pl.ds(pl.multiple_of(core * T, T), T)
        tokv[rows, cols] = (tokv[rows, cols].astype(F32) + tgr[:, cols].astype(F32)).astype(BF16)
        c_tg(p).start()

    loop(4, token_sum)

    loop(NX, lambda j: m_rax(j).wait_recv(), 1)
    mine = fin.at[xl, core]
    mine[0:HA] = add(ga.at[z, y, xh, pl.ds(pl.multiple_of(xl * HA, 16), HA)], *(rax.at[i] for i in range(3)))
    loop(NZ, lambda j: m_rcz(j).wait_recv(), 1)
    mine[HA + HB :] = add(gc.at[x, z, y], *(rcz.at[i] for i in range(7)))
    loop(NZ, lambda j: m_rbz(j).wait_recv(), 1)
    mine[HA : HA + HB] = add(gb.at[y, z, xh, xl], *(rbz.at[i] for i in range(7)))
    for i in range(3):
        m_fin(i).start()
    loop(NZ, lambda j: m_gz(j).wait_recv(), 1)
    total = add(gsend.at[2], *(grecv.at[6 + i] for i in range(7)))
    gfin[core] = jnp.broadcast_to(jnp.sum(total, axis=0, keepdims=True), (8, HALF))
    m_gs().start()

    m_ax().wait_send()

    def drain_y(j):
        m_ay(j).wait_send()
        m_ray(j).wait_send()
        m_gy(j).wait_send()

    def drain_x(j):
        m_rax(j).wait_send()
        m_gx(j).wait_send()

    def drain_z(j):
        m_bz(j).wait_send()
        m_cz(j).wait_send()
        m_rbz(j).wait_send()
        m_rcz(j).wait_send()
        m_gz(j).wait_send()

    loop(NY, drain_y, 1)
    loop(NX, drain_x, 1)
    loop(NZ, drain_z, 1)

    def drain(k):
        def inner(j):
            m_bx(k, j).wait_send()
            m_cy(k, j).wait_send()
            m_rbx(k, j).wait_send()
            m_rcy(k, j).wait_send()

        loop(4, inner, 1)
        for d in range(2):
            for hop in range(2):
                m_by(k, d, hop).wait_send()
                m_cx(k, d, hop).wait_send()
            for what in range(3):
                m_rb(k, d, what).wait_send()
                m_rc(k, d, what).wait_send()
            m_az(d, k, d).wait_send()

            @pl.when(k < 3)
            def _():
                m_az(d, k, 1 - d).wait_send()

        d_tok(k).wait_send()

    loop(4, drain)
    for d in range(2):
        for s in range(4):
            m_f(d, s, True).wait_send()
        for s in range(1, 4):
            m_n(d, s, True).wait_send()
    d_kg().wait_send()
    d_stats().wait_send()
    d_keys().wait()
    c_keys().wait()
    loop(4, lambda p: c_tg(p).wait())

    for i in range(3):
        m_fin(i).wait()
    m_gs().wait()
    for c in range(2):
        for half in range(2):
            for segs, at, size in ((SEG_A, 0, HA), (SEG_B, HA, HB), (SEG_C, HA + HB, HC)):
                for first, last, row, block in segs:
                    if first // size == half:
                        wg_out[row : row + last - first, column(4 * c + block)] = fin[
                            half, c, at + first - half * size : at + last - half * size
                        ]
        gg_out[:, c * HALF : (c + 1) * HALF] = gfin[c, 0:1]


def scratch():
    vmem, dma = pltpu.VMEM, pltpu.SemaphoreType.DMA
    both = lambda n: [dma((n,)), dma((n,))]
    buffers = [
        vmem((2 * T, D), BF16),
        vmem((D, 2 * T), BF16),
        vmem((2 * T, HALF), BF16),
        vmem((D, HALF), BF16),
        vmem((NZ, NY, 2, RA, BLOCK), BF16),
        vmem((NY, NZ, 2, 2, HB, BLOCK), BF16),
        vmem((NX, NZ, NY, HC, BLOCK), BF16),
        vmem((2 * T, HALF), F32),
        vmem((2 * T, HALF), BF16),
        vmem((2 * T, HALF), BF16),
        vmem((3, 2, 8, BLOCK), F32),
        vmem((NZ, NY, 2, RA, BLOCK), BF16),
        vmem((NY, NZ, 2, 2, HB, BLOCK), BF16),
        vmem((NX, NZ, NY, HC, BLOCK), BF16),
        vmem((2, 4, 2, 2, RA, BLOCK), BF16),
        vmem((2, 3, 2, 2, RA, BLOCK), BF16),
        vmem((4, 2, 3, 2, 2, HB, BLOCK), BF16),
        vmem((4, 2, 3, NY, HC, BLOCK), BF16),
        vmem((3, 2, RA, BLOCK), BF16),
        vmem((3, HA, BLOCK), BF16),
        vmem((3, NZ, HB, BLOCK), BF16),
        vmem((7, HB, BLOCK), BF16),
        vmem((3, NZ, HC, BLOCK), BF16),
        vmem((7, HC, BLOCK), BF16),
        vmem((T, D), BF16),
        vmem((3, 8, HALF), F32),
        vmem((13, 8, HALF), F32),
        vmem((2, 8, HALF), F32),
        vmem((2, 2, HA + HB + HC, BLOCK), F32),
        vmem((ROWS, HALF), BF16),
    ]
    semaphores = [dma((5,)), dma((5,))]
    for n in (11, 1, 3, 16, 14, 12, 12, 32, 8, 6, 48, 44, 14, 3):
        semaphores += both(n)
    return buffers + semaphores


def local(tokens, codes, scales, norm_gain, key_grad):
    hbm, vmem = pl.BlockSpec(memory_space=pl.ANY), pl.BlockSpec(memory_space=pltpu.VMEM)
    keys, token_grad, weight_grad, gain_grad = pl.pallas_call(
        kernel,
        out_shape=(
            jax.ShapeDtypeStruct((T, W), BF16),
            jax.ShapeDtypeStruct((T, D), BF16),
            jax.ShapeDtypeStruct((ROWS, W), F32),
            jax.ShapeDtypeStruct((1, W), F32),
        ),
        in_specs=[hbm, vmem, vmem, vmem, hbm],
        out_specs=(hbm, hbm, vmem, vmem),
        scratch_shapes=scratch(),
        compiler_params=pltpu.CompilerParams(collective_id=0, has_side_effects=True, vmem_limit_bytes=61 << 20),
        cost_estimate=pl.CostEstimate(flops=6 * T * D * W, bytes_accessed=12 << 20, transcendentals=0),
    )(tokens, codes, scales, norm_gain.reshape(1, W), key_grad)
    return keys, token_grad, weight_grad, gain_grad.reshape(W)


def solution(mesh):
    return jax.shard_map(
        local,
        mesh=mesh,
        in_specs=(P(("dp", "fsdp"), None), P("fsdp", None), P("fsdp", None), P(), P(("dp", "fsdp"), None)),
        out_specs=(P(("dp", "fsdp"), None), P(("dp", "fsdp"), None), P("fsdp", None), P()),
        check_vma=False,
    )
```

```python
import jax
import jax.numpy as jnp
from jax import lax
from jax.experimental import pallas as pl
from jax.experimental.pallas import tpu as pltpu
from jax.sharding import PartitionSpec as P

MESH = pl.DeviceIdType.MESH
F32, BF16 = jnp.float32, jnp.bfloat16
BLOCK = 128
EPS = 1e-06
D, W, T, ROWS = 5120, 1024, 384, 80
HALF = W // 2
SLAB = 640
PAIR = 2 * SLAB
RA, RB, RC = 96, 96, 128
GA, GB, GC = 96, 96, 128
NX, NY, NZ = 4, 4, 8
UNITS = (1, 2, 3, 0)


def segments(rows, block, offset, half):
    cuts = []
    for first, last, row, column in ((0, ROWS, 0, block), (ROWS, rows, offset, 3)):
        if first < half < last:
            cuts += [(first, half, row, column), (half, last, row + half - first, column)]
        else:
            cuts.append((first, last, row, column))
    return cuts


def parts(a, b, c):
    return (
        (segments(a, 0, 0, a // 2), a // 2),
        (segments(b, 1, a - ROWS, b // 2), b // 2),
        (segments(c, 2, a + b - 2 * ROWS, c // 2), c // 2),
    )


(SEG_A, HA), (SEG_B, HB), (SEG_C, HC) = parts(RA, RB, RC)
(SEG_GA, HGA), (SEG_GB, HGB), (SEG_GC, HGC) = parts(GA, GB, GC)


def column(block):
    return pl.ds(block * BLOCK, BLOCK)


def rem(a, n):
    return lax.rem(a + 2 * n, n)


def add(*refs):
    total = refs[0][...].astype(F32)
    for ref in refs[1:]:
        total = total + ref[...].astype(F32)
    return total


def kernel(
    tokens, codes, scales, gain, key_grad,
    keys_out, tg_out, wg_out, gg_out,
    tokv, tokt, kgv, wf, wa, wb, wc, acc, draw, keyv, stats,
    ga, gb, gc, raa, rb, rc, ray, rax, rbx, rbz, rcy, rcz, tgr, gx, gy, gz, gfin, fin, stage,
    s_loc, s_out,
    s_d2d, r_d2d, s_ax, r_ax, s_ay, r_ay, s_az, r_az, s_z, r_z, s_bx, r_bx, s_cy, r_cy, s_by, r_by, s_cx, r_cx,
    s_raa, r_raa, s_rr, r_rr, s_one, r_one, s_gain, r_gain, s_fin, r_fin,
):
    dp, fs = lax.axis_index("dp"), lax.axis_index("fsdp")
    xl, core = dp // 2, lax.rem(dp, 2)
    z, y, xh = fs // 8, lax.rem(fs // 2, 4), lax.rem(fs, 2)
    x = xh * 2 + xl
    other = 1 - core
    sign = 2 * lax.rem(z, 2) - 1

    def dev(x_, y_, z_, c_):
        x_, y_, z_ = rem(x_, NX), rem(y_, NY), rem(z_, NZ)
        return (lax.rem(x_, 2) * 2 + c_, z_ * 8 + y_ * 2 + x_ // 2)

    def copy(src, dst, send, recv, device):
        return pltpu.make_async_remote_copy(
            src_ref=src, dst_ref=dst, send_sem=send, recv_sem=recv, device_id=device, device_id_type=MESH
        )

    def pair(k):
        return rem(z // 2 + sign * (k + k // 2 - 2 * (k // 3)), 4)

    def loop(n, body, first=0):
        lax.fori_loop(first, n, lambda i, c: (body(i), c)[1], 0)

    sib = dev(x, y, z, other)

    def c_tok(p):
        cols = pl.ds(p * PAIR, PAIR)
        return pltpu.make_async_copy(tokens.at[:, cols], tokv.at[pl.ds(core * T, T), cols], s_loc.at[p])

    def d_tok(p):
        cols = pl.ds(p * PAIR, PAIR)
        return copy(tokens.at[:, cols], tokv.at[pl.ds(core * T, T), cols], s_d2d.at[p], r_d2d.at[p], sib)

    def c_kg():
        return pltpu.make_async_copy(
            key_grad.at[:, pl.ds(core * HALF, HALF)], kgv.at[pl.ds(core * T, T)], s_loc.at[4]
        )

    def d_kg():
        return copy(
            key_grad.at[:, pl.ds(other * HALF, HALF)], kgv.at[pl.ds(core * T, T)], s_d2d.at[4], r_d2d.at[4], sib
        )

    def d_stats():
        return copy(stats.at[0], stats.at[1], s_d2d.at[5], r_d2d.at[5], sib)

    def d_keys():
        return copy(
            keyv.at[pl.ds(other * T, T)], keys_out.at[:, pl.ds(core * HALF, HALF)], s_d2d.at[6], r_d2d.at[6], sib
        )

    def c_keys():
        return pltpu.make_async_copy(
            keyv.at[pl.ds(core * T, T)], keys_out.at[:, pl.ds(core * HALF, HALF)], s_out.at[4]
        )

    def d_tg(p):
        cols = pl.ds(p * PAIR, PAIR)
        return copy(tokv.at[pl.ds(other * T, T), cols], tgr.at[:, cols], s_d2d.at[7 + p], r_d2d.at[7 + p], sib)

    def m_ax():
        return copy(wa.at[z, 0, 0], wa.at[z, 1, 0], s_ax.at[0], r_ax.at[0], dev(3 - x, y, z, core))

    def m_ay(u, j):
        at = u * 3 + j - 1
        return copy(wa.at[z, u, 0], wa.at[z, u, 4 - j], s_ay.at[at], r_ay.at[at], dev(x, y + j, z, core))

    def m_az(d, s, u):
        sg = 1 - 2 * d
        ref = wa.at[rem(z - sg * s, NZ), u]
        at = (s * 2 + u) * 2 + d
        return copy(ref, ref, s_az.at[at], r_az.at[at], dev(x, y, z + sg, core))

    def m_z(part, d, hops, begin):
        sg = 1 - 2 * d
        to = rem(z - sg * begin, NZ)
        ref = wc.at[x, to, 0] if part else wb.at[y, to, 0]
        at = ((part * 2 + d) * 2 + (begin > 0)) * 2 + (begin or hops) - 1
        return copy(ref, ref, s_z.at[at], r_z.at[at], dev(x, y, z + sg * hops, core))

    def m_bx(k, j):
        zs = pl.ds(2 * pair(k), 2)
        at = k * 3 + j - 1
        return copy(wb.at[y, zs, 0], wb.at[y, zs, 4 - j], s_bx.at[at], r_bx.at[at], dev(x + j, y, z, core))

    def m_cy(k, j):
        zs = pl.ds(2 * pair(k), 2)
        at = k * 3 + j - 1
        return copy(wc.at[x, zs, 0], wc.at[x, zs, 4 - j], s_cy.at[at], r_cy.at[at], dev(x, y + j, z, core))

    def long_ring(buf, me, k, unit, d, hop):
        slots = pl.ds(1, 3) if unit else pl.ds(0, 1)
        if hop == 0:
            return buf.at[me, pl.ds(2 * pair(k), 2), slots]
        return buf.at[rem(me - 1 + 2 * d, 4), 2 * pair(k) + d, slots]

    def m_by(k, unit, d, hop):
        ref = long_ring(wb, y, k, unit, d, hop)
        at = ((k * 2 + unit) * 2 + hop) * 2 + d
        return copy(ref, ref, s_by.at[at], r_by.at[at], dev(x, y + 1 - 2 * d, z, core))

    def m_cx(k, unit, d, hop):
        ref = long_ring(wc, x, k, unit, d, hop)
        at = ((k * 2 + unit) * 2 + hop) * 2 + d
        return copy(ref, ref, s_cx.at[at], r_cx.at[at], dev(x + 1 - 2 * d, y, z, core))

    def far(d, u):
        return u % 2 == 1 - d

    def m_a(d, u, s, first=False):
        sg = 1 - 2 * d
        src = ga.at[rem(z + sg * (4 - s), NZ), u] if first else raa.at[d, u, s - 1]
        at = (d * 4 + u) * 4 + s
        return copy(src, raa.at[d, u, s], s_raa.at[at], r_raa.at[at], dev(x, y, z + sg, core))

    def m_rb(k, d, what):
        sg = 1 - 2 * d
        q = pair(3 - k)
        src = (
            gb.at[rem(y + 2, NY), 2 * q + d],
            gb.at[rem(y + sg, NY), 2 * q + 1 - d],
            rb.at[k, d, 0],
        )[what]
        at = (k * 2 + d) * 3 + what
        return copy(src, rb.at[k, d, what], s_rr.at[at], r_rr.at[at], dev(x, y + sg, z, core))

    def m_rc(k, d, what):
        sg = 1 - 2 * d
        q = pair(3 - k)
        src = (
            gc.at[rem(x + 2, NX), 2 * q + d],
            gc.at[rem(x + sg, NX), 2 * q + 1 - d],
            rc.at[k, d, 0],
        )[what]
        at = 24 + (k * 2 + d) * 3 + what
        return copy(src, rc.at[k, d, what], s_rr.at[at], r_rr.at[at], dev(x + sg, y, z, core))

    def m_rbx(k, j):
        to = rem(x + j, NX)
        zs = pl.ds(2 * pair(3 - k), 2)
        at = k * 3 + j - 1
        return copy(
            gb.at[y, zs, to // 2, lax.rem(to, 2)], rbx.at[j - 1, zs], s_one.at[at], r_one.at[at], dev(to, y, z, core)
        )

    def m_rcy(k, j):
        to = rem(y + j, NY)
        zs = pl.ds(2 * pair(3 - k), 2)
        at = 12 + k * 3 + j - 1
        return copy(gc.at[x, zs, to], rcy.at[j - 1, zs], s_one.at[at], r_one.at[at], dev(x, to, z, core))

    def m_rz(part, d, s, first=False):
        sg = 1 - 2 * d
        to = rem(z + sg * (4 - s), NZ)
        own, held = (gc.at[x, to, y], rcz) if part else (gb.at[y, to, xh, xl], rbz)
        at = 24 + (part * 2 + d) * 4 + s
        return copy(own if first else held.at[d, s - 1], held.at[d, s], s_one.at[at], r_one.at[at], dev(x, y, z + sg, core))

    def m_ray(j):
        to = rem(y + j, NY)
        at = 39 + j
        return copy(ga.at[z, j], ray.at[j - 1], s_one.at[at], r_one.at[at], dev(x, to, z, core))

    def m_rax(j):
        to = rem(x + j, NX)
        at = 42 + j
        src = ga.at[z, 0, to // 2, pl.ds(lax.rem(to, 2) * HGA, HGA)]
        return copy(src, rax.at[j - 1], s_one.at[at], r_one.at[at], dev(to, y, z, core))

    def m_gx(j):
        ref = gx.at[x]
        return copy(ref, ref, s_gain.at[j - 1], r_gain.at[j - 1], dev(x + j, y, z, core))

    def m_gy(j):
        ref = gy.at[y]
        return copy(ref, ref, s_gain.at[2 + j], r_gain.at[2 + j], dev(x, y + j, z, core))

    def m_gz(d, s):
        sg = 1 - 2 * d
        ref = gz.at[rem(z - sg * s, NZ)]
        at = 6 + d * 4 + s
        return copy(ref, ref, s_gain.at[at], r_gain.at[at], dev(x, y, z + sg, core))

    def m_gs():
        return copy(gfin.at[core], gfin.at[core], s_gain.at[14], r_gain.at[14], sib)

    partner = x + 1 - 2 * xl
    fins = (dev(partner, y, z, core), sib, dev(partner, y, z, other))

    def m_fin(i):
        return copy(fin.at[xl, core], fin.at[xl, core], s_fin.at[i], r_fin.at[i], fins[i])

    loop(4, lambda p: c_tok(p).start())
    c_kg().start()

    barrier = pltpu.get_barrier_semaphore()

    def signal(device):
        pl.semaphore_signal(barrier, inc=1, device_id=device, device_id_type=MESH)

    loop(NX, lambda j: signal(dev(x + j, y, z, core)), 1)
    loop(NY, lambda j: signal(dev(x, y + j, z, core)), 1)
    for hops in (1, 2):
        signal(dev(x, y, z + hops, core))
        signal(dev(x, y, z - hops, core))
    signal(sib)
    signal(fins[2])

    scale_t = scales[...].T
    for b in range(4):
        scale = jnp.where(core == 0, scale_t[:, b : b + 1], scale_t[:, 4 + b : 5 + b])
        code = codes[:, pl.ds(pl.multiple_of(core * HALF + b * BLOCK, BLOCK), BLOCK)]
        stage[:, column(b)] = (code.astype(F32) * scale).astype(BF16)
    for first, last, row, block in SEG_A:
        wa[z, 0, 0, first:last] = stage[row : row + last - first, column(block)]
    for mine in range(2):

        @pl.when(xl == mine)
        def _():
            for first, last, row, block in SEG_B:
                if first // HB == mine:
                    wb[y, z, 0, first - mine * HB : last - mine * HB] = stage[row : row + last - first, column(block)]
            for first, last, row, block in SEG_C:
                if first // HC == mine:
                    wc[x, z, 0, first - mine * HC : last - mine * HC] = stage[row : row + last - first, column(block)]

    pl.semaphore_wait(barrier, 12)
    m_ax().start()
    for j in range(1, NY):
        m_ay(0, j).start()
    for part in (1, 0):
        for hops in (2, 1):
            for d in range(2):
                m_z(part, d, hops, 0).start()
    d_kg().start()
    loop(4, lambda k: d_tok(pair(k)).start())
    acc[...] = jnp.zeros_like(acc)
    loop(4, lambda p: c_tok(p).wait())
    c_kg().wait()
    d_kg().wait_recv()

    def consume(k):
        p = pair(k)

        def rows_of(i):
            zz, yy, hh = 2 * p + i // 8, lax.rem(i // 2, 4), lax.rem(i, 2)
            base = zz * SLAB + yy * 160 + hh * ROWS
            for first, last, row, block in SEG_A:
                wf[pl.ds(pl.multiple_of(base + row, 16), last - first), column(block)] = wa[
                    zz, (hh + xh) % 2, rem(yy - y, NY), first:last
                ]
            for first, last, row, block in SEG_B:
                at = first // HB
                wf[pl.ds(pl.multiple_of(base + row, 16), last - first), column(block)] = wb[
                    yy, zz, rem(2 * hh + at - x, NX), first - at * HB : last - at * HB
                ]
            for first, last, row, block in SEG_C:
                at = first // HC
                wf[pl.ds(pl.multiple_of(base + row, 16), last - first), column(block)] = wc[
                    2 * hh + at, zz, rem(yy - y, NY), first - at * HC : last - at * HC
                ]

        loop(16, rows_of)
        begin = pl.multiple_of(p * PAIR, BLOCK)
        acc[...] += jnp.dot(tokv[:, pl.ds(begin, PAIR)], wf[pl.ds(begin, PAIR), :], preferred_element_type=F32)

    def transpose(k):
        d_tok(pair(k)).wait_recv()

        def part(i):
            begin = pl.multiple_of(pair(k) * PAIR + i * 256, BLOCK)
            tokt[pl.ds(begin, 256), :] = tokv[:, pl.ds(begin, 256)].T

        loop(5, part)

    def own_columns(part, ks):
        for k in ks:
            for d in range(2):
                (m_cx if part else m_by)(k, 0, d, 0).start()
            for j in range(1, 4):
                (m_cy if part else m_bx)(k, j).start()

    def far_z(part, wait):
        for d, begin in ((0, 1), (1, 1), (1 - part, 2)):
            move = m_z(part, d, 2, begin)
            move.wait_recv() if wait else move.start()

    def columns(k):
        for j in range(1, NY):
            m_cy(k, j).wait_recv()
        for d in range(2):
            m_cx(k, 1, d, 0).start()
        for j in range(1, NX):
            m_bx(k, j).wait_recv()
        for d in range(2):
            m_by(k, 1, d, 0).start()

    def own_forward(k):
        for d in range(2):
            m_cx(k, 0, d, 0).wait_recv()
            m_cx(k, 0, d, 1).start()
            m_by(k, 0, d, 0).wait_recv()
            m_by(k, 0, d, 1).start()

    m_ax().wait_recv()
    for j in range(1, NY):
        m_ay(1, j).start()
    for part in (1, 0):
        for hops in (1, 2):
            for d in range(2):
                m_z(part, d, hops, 0).wait_recv()
        far_z(part, False)
        own_columns(part, (0, 1))
    for j in range(1, NY):
        m_ay(0, j).wait_recv()
    for d in range(2):
        m_az(d, 0, 0).start()
    far_z(1, True)
    own_columns(1, (2, 3))
    far_z(0, True)
    own_columns(0, (2, 3))
    for j in range(1, NY):
        m_ay(1, j).wait_recv()
    for d in range(2):
        m_az(d, 0, 1).start()
    for d in range(2):
        m_az(d, 0, 0).wait_recv()
        m_az(d, 1, 0).start()
    loop(2, columns)
    loop(2, own_forward)
    for d in range(2):
        m_az(d, 0, 1).wait_recv()
        m_az(d, 1, 1).start()

    def forward(k):
        for d in range(2):
            m_cx(k, 1, d, 0).wait_recv()
            m_cx(k, 1, d, 1).start()
            m_by(k, 1, d, 0).wait_recv()
            m_by(k, 1, d, 1).start()

    def later(k):
        columns(k)
        forward(k - 2)
        own_forward(k)

    loop(4, later, 2)

    def ring(k):
        for u in range(2):
            for d in range(2):

                @pl.when(k < 2 + (u == d))
                def _():
                    m_az(d, k + 1, u).wait_recv()

                @pl.when(k < 1 + (u == d))
                def _():
                    m_az(d, k + 2, u).start()

        @pl.when(k < 2)
        def _():
            forward(k + 2)

        transpose(k)

        @pl.when(k > 0)
        def _():
            last_hops(k - 1)
            consume(k - 1)

    def last_hops(k):
        for unit in range(2):
            for d in range(2):
                m_cx(k, unit, d, 1).wait_recv()
                m_by(k, unit, d, 1).wait_recv()

    loop(4, ring)
    last_hops(3)
    consume(3)

    gains = gain[0:1, pl.ds(pl.multiple_of(core * HALF, BLOCK), HALF)]
    lane = lax.broadcasted_iota(jnp.int32, (8, BLOCK), 1)
    CH = 64

    def sums(i, packed):
        rows = pl.ds(pl.multiple_of(i * CH, CH), CH)
        k_raw = acc[rows, :]
        dn = kgv[rows, :].astype(F32) * gains
        one = jnp.sum(k_raw * k_raw, axis=1, keepdims=True)
        two = jnp.sum(dn * k_raw, axis=1, keepdims=True)
        for j in range(CH // 8):
            here = lane == i * (CH // 8) + j
            packed = (
                jnp.where(here, one[8 * j : 8 * j + 8], packed[0]),
                jnp.where(here, two[8 * j : 8 * j + 8], packed[1]),
            )
        return packed

    nothing = jnp.zeros((8, BLOCK), F32)
    stats[0, 0], stats[0, 1] = lax.fori_loop(0, 2 * T // CH, sums, (nothing, nothing))
    d_stats().start()
    d_stats().wait_recv()
    stats[2] = (stats[0] + stats[1]) * (1.0 / W)
    gx[x] = jnp.zeros((8, HALF), F32)

    def factors(i):
        rinvs, means = [], []
        for j in range(CH // 8):
            here = lane == i * (CH // 8) + j
            rinv = lax.rsqrt(jnp.sum(jnp.where(here, stats[2, 0], 0.0), axis=1, keepdims=True) + EPS)
            rinvs.append(rinv)
            means.append(rinv * jnp.sum(jnp.where(here, stats[2, 1], 0.0), axis=1, keepdims=True))
        return jnp.concatenate(rinvs, axis=0), jnp.concatenate(means, axis=0)

    def norm(i):
        rows = pl.ds(pl.multiple_of(i * CH, CH), CH)
        rinv, mean = factors(i)
        draw[rows, :] = (rinv * (kgv[rows, :].astype(F32) * gains - acc[rows, :] * (rinv * mean))).astype(BF16)

    loop(2 * T // CH, norm)

    def norm_keys(i):
        rows = pl.ds(pl.multiple_of(i * CH, CH), CH)
        normed = acc[rows, :] * factors(i)[0]
        keyv[rows, :] = (normed * gains).astype(BF16)
        gx[x] += jnp.sum((kgv[rows, :].astype(F32) * normed).reshape(CH // 8, 8, HALF), axis=0)

    def grad(t):
        k = t // 2
        e = rem(z + t, 2)
        zz = 2 * pair(3 - k) + e
        begin = pl.multiple_of(zz * SLAB, BLOCK)
        part = jnp.dot(tokt[pl.ds(begin, SLAB), :], draw[...], preferred_element_type=F32).astype(BF16)
        for yy in range(NY):
            for hh in range(2):
                base = yy * 160 + hh * ROWS
                for first, last, row, block in SEG_GA:
                    value = part[base + row : base + row + last - first, block * BLOCK : (block + 1) * BLOCK]
                    ga[zz, rem(yy - y, NY), hh, first:last] = value
                for first, last, row, block in SEG_GB:
                    value = part[base + row : base + row + last - first, block * BLOCK : (block + 1) * BLOCK]
                    at = first // HGB
                    gb[yy, zz, hh, at, first - at * HGB : last - at * HGB] = value
                for first, last, row, block in SEG_GC:
                    value = part[base + row : base + row + last - first, block * BLOCK : (block + 1) * BLOCK]
                    at = first // HGC
                    gc[2 * hh + at, zz, yy, first - at * HGC : last - at * HGC] = value

        @pl.when(k < 2)
        def _():
            m_rc(k, e, 0).start()
            m_rb(k, e, 0).start()
            m_rc(k, 1 - e, 1).start()
            m_rb(k, 1 - e, 1).start()

        @pl.when(t == 0)
        def _():
            for u in UNITS:
                m_a(u % 2 ^ 1, u, 0, True).start()

        for at, d in ((1, 1 - lax.rem(z, 2)), (3, lax.rem(z, 2))):

            @pl.when(t == at)
            def _():
                for i in range(2):
                    m_a(d, d + 2 * i, 1, True).start()

    loop(8, grad)
    loop(2 * T // CH, norm_keys)
    d_keys().start()
    c_keys().start()
    loop(NX, lambda j: m_gx(j).start(), 1)

    def finish(k):
        q = pair(3 - k)
        for d in range(2):
            m_rc(k, d, 1).wait_recv()
            m_rc(k, d, 2).wait_recv()
        for h in range(2):
            ref = gc.at[x, 2 * q + h]
            ref[...] += rc[k, h, 2] + rc[k, 1 - h, 1]
        loop(NY, lambda j: m_rcy(k, j).start(), 1)
        for d in range(2):
            m_rb(k, d, 1).wait_recv()
            m_rb(k, d, 2).wait_recv()
        for h in range(2):
            ref = gb.at[y, 2 * q + h]
            ref[...] += rb[k, h, 2] + rb[k, 1 - h, 1]
        loop(NX, lambda j: m_rbx(k, j).start(), 1)

    def short(k):
        for j in range(1, NY):
            m_rcy(k, j).wait_recv()
            m_rbx(k, j).wait_recv()

        def slab(i):
            zz = 2 * pair(3 - k) + i
            ref = gc.at[x, zz, y]
            ref[...] = add(ref, *(rcy.at[i, zz] for i in range(3))).astype(BF16)
            ref = gb.at[y, zz, xh, xl]
            ref[...] = add(ref, *(rbx.at[i, zz] for i in range(3))).astype(BF16)

        loop(2, slab)
        for part, d in ((1, 0), (1, 1), (0, 0), (0, 1)):
            begin = 0 if part != d else 1
            to = rem(z + (1 - 2 * d) * (4 - k), NZ)

            @pl.when(k == begin)
            def _():
                m_rz(part, d, begin, True).start()

            @pl.when(k > begin)
            def _():
                m_rz(part, d, k - 1, True).wait_recv()
                if part:
                    rcz[d, k - 1] += gc[x, to, y]
                else:
                    rbz[d, k - 1] += gb[y, to, xh, xl]
                m_rz(part, d, k).start()

    def token_part(p):
        begin = pl.multiple_of(p * PAIR, BLOCK)
        weight = wf[pl.ds(begin, PAIR), :]
        for to in (other, core):
            rows = pl.ds(pl.multiple_of(to * T, T), T)
            tokv[rows, pl.ds(begin, PAIR)] = lax.dot_general(
                draw[rows, :], weight, (((1,), (1,)), ((), ())), preferred_element_type=F32
            ).astype(BF16)
        d_tg(p).start()

    def gain_step(s):
        for d in range(2):
            m_gz(d, s).wait_recv()
            m_gz(d, s + 1).start()

    def reduce(k):
        for d in range(2):
            sg = 1 - 2 * d
            q = pair(3 - k)
            m_rc(k, d, 0).wait_recv()
            ref = rc.at[k, d, 0]
            ref[...] += gc[rem(x + sg, NX), 2 * q + d]
            m_rc(k, d, 2).start()
            m_rb(k, d, 0).wait_recv()
            ref = rb.at[k, d, 0]
            ref[...] += gb[rem(y + sg, NY), 2 * q + d]
            m_rb(k, d, 2).start()

        @pl.when(k < 2)
        def _():
            for what in range(2):
                for d in range(2):
                    m_rc(k + 2, d, what).start()
                    m_rb(k + 2, d, what).start()

        for u in UNITS:
            for d in range(2):
                sg = 1 - 2 * d

                @pl.when((k < 3) & (k >= (0 if far(d, u) else 1)))
                def _():
                    m_a(d, u, k, True).wait_recv()
                    raa[d, u, k] += ga[rem(z + sg * (3 - k), NZ), u]
                    m_a(d, u, k + 1).start()

        token_part(k)

        @pl.when(k > 0)
        def _():
            finish(k - 1)

        @pl.when(k > 1)
        def _():
            short(k - 2)

        @pl.when(k == 0)
        def _():
            loop(NX, lambda j: m_gx(j).wait_recv(), 1)
            gy[y] = add(*(gx.at[i] for i in range(NX)))
            loop(NY, lambda j: m_gy(j).start(), 1)

        @pl.when(k == 1)
        def _():
            loop(NY, lambda j: m_gy(j).wait_recv(), 1)
            gz[z] = add(*(gy.at[i] for i in range(NY)))
            for d in range(2):
                m_gz(d, 0).start()

        @pl.when(k > 1)
        def _():
            gain_step(k - 2)

    loop(4, reduce)
    m_gz(0, 2).wait_recv()
    m_gz(1, 2).wait_recv()
    m_gz(0, 3).start()
    finish(3)
    short(2)
    for u in UNITS:
        for d in range(2):
            m_a(d, u, 3, True).wait_recv()
        ref = ga.at[z, u]
        ref[...] += raa[0, u, 3] + raa[1, u, 3]
        if u > 0:
            m_ray(u).start()

    loop(NY, lambda j: m_ray(j).wait_recv(), 1)
    ref = ga.at[z, 0]
    ref[...] = add(ref, *(ray.at[i] for i in range(3))).astype(BF16)
    loop(NX, lambda j: m_rax(j).start(), 1)
    short(3)

    m_gz(0, 3).wait_recv()
    total = add(*(gz.at[i] for i in range(NZ)))
    gfin[core] = jnp.broadcast_to(jnp.sum(total, axis=0, keepdims=True), (8, HALF))
    m_gs().start()

    def token_sum(p):
        d_tg(p).wait()
        begin = pl.multiple_of(p * PAIR, BLOCK)
        cols = pl.ds(begin, PAIR)
        rows = pl.ds(pl.multiple_of(core * T, T), T)
        tg_out[:, cols] = (tokv[rows, cols].astype(F32) + tgr[:, cols].astype(F32)).astype(BF16)

    loop(4, token_sum)

    loop(NX, lambda j: m_rax(j).wait_recv(), 1)
    mine = fin.at[xl, core]
    own = ga.at[z, 0, xh, pl.ds(pl.multiple_of(xl * HGA, 16), HGA)]
    mine[0:HGA] = add(own, *(rax.at[i] for i in range(3))).astype(BF16)
    for d in range(2):
        m_rz(1, d, 3).wait_recv()
    mine[HGA + HGB :] = add(gc.at[x, z, y], rcz.at[0, 3], rcz.at[1, 3]).astype(BF16)
    for d in range(2):
        m_rz(0, d, 3).wait_recv()
    mine[HGA : HGA + HGB] = add(gb.at[y, z, xh, xl], rbz.at[0, 3], rbz.at[1, 3]).astype(BF16)
    for i in range(3):
        m_fin(i).start()
    m_ax().wait_send()

    def drain_y(j):
        m_ray(j).wait_send()
        m_gy(j).wait_send()

    def drain_x(j):
        m_rax(j).wait_send()
        m_gx(j).wait_send()

    loop(NY, drain_y, 1)
    loop(NX, drain_x, 1)

    def drain(k):
        def inner(j):
            m_bx(k, j).wait_send()
            m_cy(k, j).wait_send()
            m_rbx(k, j).wait_send()
            m_rcy(k, j).wait_send()

        loop(4, inner, 1)
        for d in range(2):
            for hop in range(2):
                for unit in range(2):
                    m_by(k, unit, d, hop).wait_send()
                    m_cx(k, unit, d, hop).wait_send()
            for what in range(3):
                m_rb(k, d, what).wait_send()
                m_rc(k, d, what).wait_send()
            for u in range(2):

                @pl.when(k < 3 + (u == d))
                def _():
                    m_az(d, k, u).wait_send()

            for u in range(4):

                @pl.when(k >= (0 if far(d, u) else 1))
                def _():
                    m_a(d, u, k, True).wait_send()

            @pl.when(k < 4 - d)
            def _():
                m_gz(d, k).wait_send()

            @pl.when(k >= d)
            def _():
                m_rz(1, d, k, True).wait_send()

            @pl.when(k >= 1 - d)
            def _():
                m_rz(0, d, k, True).wait_send()

        d_tok(k).wait_send()

    loop(4, drain)
    for u in range(2):
        for j in range(1, NY):
            m_ay(u, j).wait_send()
    for part in range(2):
        for d, hops, begin in ((0, 1, 0), (1, 1, 0), (0, 2, 0), (1, 2, 0), (0, 2, 1), (1, 2, 1), (1 - part, 2, 2)):
            m_z(part, d, hops, begin).wait_send()
    d_kg().wait_send()
    d_stats().wait_send()
    d_keys().wait()
    c_keys().wait()

    for i in range(3):
        m_fin(i).wait()
    m_gs().wait()
    for c in range(2):
        for half in range(2):
            for segs, at, size in ((SEG_GA, 0, HGA), (SEG_GB, HGA, HGB), (SEG_GC, HGA + HGB, HGC)):
                for first, last, row, block in segs:
                    if first // size == half:
                        wg_out[row : row + last - first, column(4 * c + block)] = fin[
                            half, c, at + first - half * size : at + last - half * size
                        ].astype(F32)
        gg_out[:, c * HALF : (c + 1) * HALF] = gfin[c, 0:1]


def scratch():
    vmem, dma = pltpu.VMEM, pltpu.SemaphoreType.DMA
    both = lambda n: [dma((n,)), dma((n,))]
    buffers = [
        vmem((2 * T, D), BF16),
        vmem((D, 2 * T), BF16),
        vmem((2 * T, HALF), BF16),
        vmem((D, HALF), BF16),
        vmem((NZ, 2, NY, RA, BLOCK), BF16),
        vmem((NY, NZ, NX, HB, BLOCK), BF16),
        vmem((NX, NZ, NY, HC, BLOCK), BF16),
        vmem((2 * T, HALF), F32),
        vmem((2 * T, HALF), BF16),
        vmem((2 * T, HALF), BF16),
        vmem((3, 2, 8, BLOCK), F32),
        vmem((NZ, NY, 2, GA, BLOCK), BF16),
        vmem((NY, NZ, 2, 2, HGB, BLOCK), BF16),
        vmem((NX, NZ, NY, HGC, BLOCK), BF16),
        vmem((2, 4, 4, 2, GA, BLOCK), BF16),
        vmem((4, 2, 3, 2, 2, HGB, BLOCK), BF16),
        vmem((4, 2, 3, NY, HGC, BLOCK), BF16),
        vmem((3, 2, GA, BLOCK), BF16),
        vmem((3, HGA, BLOCK), BF16),
        vmem((3, NZ, HGB, BLOCK), BF16),
        vmem((2, 4, HGB, BLOCK), BF16),
        vmem((3, NZ, HGC, BLOCK), BF16),
        vmem((2, 4, HGC, BLOCK), BF16),
        vmem((T, D), BF16),
        vmem((NX, 8, HALF), F32),
        vmem((NY, 8, HALF), F32),
        vmem((NZ, 8, HALF), F32),
        vmem((2, 8, HALF), F32),
        vmem((2, 2, HGA + HGB + HGC, BLOCK), BF16),
        vmem((ROWS, HALF), BF16),
    ]
    semaphores = [dma((5,)), dma((5,))]
    for n in (11, 1, 6, 16, 16, 12, 12, 32, 32, 32, 48, 46, 15, 3):
        semaphores += both(n)
    return buffers + semaphores


def local(tokens, codes, scales, norm_gain, key_grad):
    hbm, vmem = pl.BlockSpec(memory_space=pl.ANY), pl.BlockSpec(memory_space=pltpu.VMEM)
    keys, token_grad, weight_grad, gain_grad = pl.pallas_call(
        kernel,
        out_shape=(
            pltpu.VMEM((T, W), BF16),
            pltpu.VMEM((T, D), BF16),
            pltpu.VMEM((ROWS, W), F32),
            pltpu.VMEM((1, W), F32),
        ),
        in_specs=[hbm, vmem, vmem, vmem, hbm],
        out_specs=(vmem, vmem, vmem, vmem),
        scratch_shapes=scratch(),
        compiler_params=pltpu.CompilerParams(collective_id=0, has_side_effects=True, vmem_limit_bytes=58 << 20),
        cost_estimate=pl.CostEstimate(flops=6 * T * D * W, bytes_accessed=12 << 20, transcendentals=0),
    )(tokens, codes, scales.T, norm_gain.reshape(1, W), key_grad)
    return keys, token_grad, weight_grad, gain_grad.reshape(W)


def solution(mesh):
    return jax.shard_map(
        local,
        mesh=mesh,
        in_specs=(P(("dp", "fsdp"), None), P("fsdp", None), P("fsdp", None), P(), P(("dp", "fsdp"), None)),
        out_specs=(P(("dp", "fsdp"), None), P(("dp", "fsdp"), None), P("fsdp", None), P()),
        check_vma=False,
    )
```

```python
import jax
import jax.numpy as jnp
from jax import lax
from jax.experimental import pallas as pl
from jax.experimental.pallas import tpu as pltpu
from jax.sharding import PartitionSpec as P

MESH = pl.DeviceIdType.MESH
F32, BF16 = jnp.float32, jnp.bfloat16
BLOCK = 128
EPS = 1e-06
D, W, T, ROWS = 5120, 1024, 384, 80
HALF = W // 2
SLAB = 640
PAIR = 2 * SLAB
RA, RB, RC = 96, 96, 128
GA, GB, GC = 96, 128, 96
NX, NY, NZ = 4, 4, 8
UNITS = (1, 2, 3, 0)


def segments(rows, block, offset, half):
    cuts = []
    for first, last, row, column in ((0, ROWS, 0, block), (ROWS, rows, offset, 3)):
        if first < half < last:
            cuts += [(first, half, row, column), (half, last, row + half - first, column)]
        else:
            cuts.append((first, last, row, column))
    return cuts


def parts(a, b, c):
    return (
        (segments(a, 0, 0, a // 2), a // 2),
        (segments(b, 1, a - ROWS, b // 2), b // 2),
        (segments(c, 2, a + b - 2 * ROWS, c // 2), c // 2),
    )


(SEG_A, HA), (SEG_B, HB), (SEG_C, HC) = parts(RA, RB, RC)
(SEG_GA, HGA), (SEG_GB, HGB), (SEG_GC, HGC) = parts(GA, GB, GC)


def column(block):
    return pl.ds(block * BLOCK, BLOCK)


def rem(a, n):
    return lax.rem(a + 2 * n, n)


def add(*refs):
    total = refs[0][...].astype(F32)
    for ref in refs[1:]:
        total = total + ref[...].astype(F32)
    return total


def kernel(
    tokens, codes, scales, gain, key_grad,
    keys_out, tg_out, wg_out, gg_out,
    tokv, tokt, kgv, wf, wa, wb, wc, acc, draw, keyv, stats,
    ga, gb, gc, raa, rb, rc, ray, rax, rbx, rbz, rcy, rcz, tgr, gx, gy, gz, gfin, fin, stage,
    s_loc, s_out,
    s_d2d, r_d2d, s_ax, r_ax, s_ay, r_ay, s_az, r_az, s_z, r_z, s_bx, r_bx, s_cy, r_cy, s_by, r_by, s_cx, r_cx,
    s_raa, r_raa, s_rr, r_rr, s_one, r_one, s_gain, r_gain, s_fin, r_fin,
):
    dp, fs = lax.axis_index("dp"), lax.axis_index("fsdp")
    xl, core = dp // 2, lax.rem(dp, 2)
    z, y, xh = fs // 8, lax.rem(fs // 2, 4), lax.rem(fs, 2)
    x = xh * 2 + xl
    other = 1 - core
    sign = 2 * lax.rem(z, 2) - 1

    def dev(x_, y_, z_, c_):
        x_, y_, z_ = rem(x_, NX), rem(y_, NY), rem(z_, NZ)
        return (lax.rem(x_, 2) * 2 + c_, z_ * 8 + y_ * 2 + x_ // 2)

    def copy(src, dst, send, recv, device):
        return pltpu.make_async_remote_copy(
            src_ref=src, dst_ref=dst, send_sem=send, recv_sem=recv, device_id=device, device_id_type=MESH
        )

    def pair(k):
        return rem(z // 2 + sign * (k + k // 2 - 2 * (k // 3)), 4)

    def loop(n, body, first=0):
        lax.fori_loop(first, n, lambda i, c: (body(i), c)[1], 0)

    sib = dev(x, y, z, other)

    def c_tok(p):
        cols = pl.ds(p * PAIR, PAIR)
        return pltpu.make_async_copy(tokens.at[:, cols], tokv.at[pl.ds(core * T, T), cols], s_loc.at[p])

    def d_tok(p):
        cols = pl.ds(p * PAIR, PAIR)
        return copy(tokens.at[:, cols], tokv.at[pl.ds(core * T, T), cols], s_d2d.at[p], r_d2d.at[p], sib)

    def c_kg():
        return pltpu.make_async_copy(
            key_grad.at[:, pl.ds(core * HALF, HALF)], kgv.at[pl.ds(core * T, T)], s_loc.at[4]
        )

    def d_kg():
        return copy(
            key_grad.at[:, pl.ds(other * HALF, HALF)], kgv.at[pl.ds(core * T, T)], s_d2d.at[4], r_d2d.at[4], sib
        )

    def d_stats():
        return copy(stats.at[0], stats.at[1], s_d2d.at[5], r_d2d.at[5], sib)

    def d_keys():
        return copy(
            keyv.at[pl.ds(other * T, T)], keys_out.at[:, pl.ds(core * HALF, HALF)], s_d2d.at[6], r_d2d.at[6], sib
        )

    def c_keys():
        return pltpu.make_async_copy(
            keyv.at[pl.ds(core * T, T)], keys_out.at[:, pl.ds(core * HALF, HALF)], s_out.at[4]
        )

    def d_tg(p):
        cols = pl.ds(p * PAIR, PAIR)
        return copy(tokv.at[pl.ds(other * T, T), cols], tgr.at[:, cols], s_d2d.at[7 + p], r_d2d.at[7 + p], sib)

    def m_ax():
        return copy(wa.at[z, 0, 0], wa.at[z, 1, 0], s_ax.at[0], r_ax.at[0], dev(3 - x, y, z, core))

    def m_ay(u, j):
        at = u * 3 + j - 1
        return copy(wa.at[z, u, 0], wa.at[z, u, 4 - j], s_ay.at[at], r_ay.at[at], dev(x, y + j, z, core))

    def m_az(d, s, u):
        sg = 1 - 2 * d
        ref = wa.at[rem(z - sg * s, NZ), u // 2, pl.ds(2 * (u % 2), 2)]
        at = (s * 4 + u) * 2 + d
        return copy(ref, ref, s_az.at[at], r_az.at[at], dev(x, y, z + sg, core))

    def m_z(part, d, hops, begin):
        sg = 1 - 2 * d
        to = rem(z - sg * begin, NZ)
        ref = wc.at[x, to, 0] if part else wb.at[y, to, 0]
        at = ((part * 2 + d) * 2 + (begin > 0)) * 2 + (begin or hops) - 1
        return copy(ref, ref, s_z.at[at], r_z.at[at], dev(x, y, z + sg * hops, core))

    def m_bx(k, j):
        zs = pl.ds(2 * pair(k), 2)
        at = k * 3 + j - 1
        return copy(wb.at[y, zs, 0], wb.at[y, zs, 4 - j], s_bx.at[at], r_bx.at[at], dev(x + j, y, z, core))

    def m_cy(k, j):
        zs = pl.ds(2 * pair(k), 2)
        at = k * 3 + j - 1
        return copy(wc.at[x, zs, 0], wc.at[x, zs, 4 - j], s_cy.at[at], r_cy.at[at], dev(x, y + j, z, core))

    def long_ring(buf, me, k, unit, d, hop):
        slots = pl.ds(1, 3) if unit else pl.ds(0, 1)
        if hop == 0:
            return buf.at[me, pl.ds(2 * pair(k), 2), slots]
        return buf.at[rem(me - 1 + 2 * d, 4), 2 * pair(k) + d, slots]

    def m_by(k, unit, d, hop):
        ref = long_ring(wb, y, k, unit, d, hop)
        at = ((k * 2 + unit) * 2 + hop) * 2 + d
        return copy(ref, ref, s_by.at[at], r_by.at[at], dev(x, y + 1 - 2 * d, z, core))

    def m_cx(k, unit, d, hop):
        ref = long_ring(wc, x, k, unit, d, hop)
        at = ((k * 2 + unit) * 2 + hop) * 2 + d
        return copy(ref, ref, s_cx.at[at], r_cx.at[at], dev(x + 1 - 2 * d, y, z, core))

    def far(d, u):
        return u % 2 == 1 - d

    def m_a(d, u, s, first=False):
        sg = 1 - 2 * d
        src = ga.at[rem(z + sg * (4 - s), NZ), u] if first else raa.at[d, u, s - 1]
        at = (d * 4 + u) * 4 + s
        return copy(src, raa.at[d, u, s], s_raa.at[at], r_raa.at[at], dev(x, y, z + sg, core))

    def m_rb(k, d, what):
        sg = 1 - 2 * d
        q = pair(3 - k)
        src = (
            gb.at[rem(y + 2, NY), 2 * q + d],
            gb.at[rem(y + sg, NY), 2 * q + 1 - d],
            rb.at[k, d, 0],
        )[what]
        at = (k * 2 + d) * 3 + what
        return copy(src, rb.at[k, d, what], s_rr.at[at], r_rr.at[at], dev(x, y + sg, z, core))

    def m_rc(k, d, what):
        sg = 1 - 2 * d
        q = pair(3 - k)
        src = (
            gc.at[rem(x + 2, NX), 2 * q + d],
            gc.at[rem(x + sg, NX), 2 * q + 1 - d],
            rc.at[k, d, 0],
        )[what]
        at = 24 + (k * 2 + d) * 3 + what
        return copy(src, rc.at[k, d, what], s_rr.at[at], r_rr.at[at], dev(x + sg, y, z, core))

    def m_rbx(k, j):
        to = rem(x + j, NX)
        zs = pl.ds(2 * pair(3 - k), 2)
        at = k * 3 + j - 1
        return copy(
            gb.at[y, zs, to // 2, lax.rem(to, 2)], rbx.at[j - 1, zs], s_one.at[at], r_one.at[at], dev(to, y, z, core)
        )

    def m_rcy(k, j):
        to = rem(y + j, NY)
        zs = pl.ds(2 * pair(3 - k), 2)
        at = 12 + k * 3 + j - 1
        return copy(gc.at[x, zs, to], rcy.at[j - 1, zs], s_one.at[at], r_one.at[at], dev(x, to, z, core))

    def m_rz(part, d, s, first=False):
        sg = 1 - 2 * d
        to = rem(z + sg * (4 - s), NZ)
        own, held = (gc.at[x, to, y], rcz) if part else (gb.at[y, to, xh, xl], rbz)
        at = 24 + (part * 2 + d) * 4 + s
        return copy(own if first else held.at[d, s - 1], held.at[d, s], s_one.at[at], r_one.at[at], dev(x, y, z + sg, core))

    def m_ray(j):
        to = rem(y + j, NY)
        at = 39 + j
        return copy(ga.at[z, j], ray.at[j - 1], s_one.at[at], r_one.at[at], dev(x, to, z, core))

    def m_rax(j):
        to = rem(x + j, NX)
        at = 42 + j
        src = ga.at[z, 0, to // 2, pl.ds(lax.rem(to, 2) * HGA, HGA)]
        return copy(src, rax.at[j - 1], s_one.at[at], r_one.at[at], dev(to, y, z, core))

    def m_gx(j):
        ref = gx.at[x]
        return copy(ref, ref, s_gain.at[j - 1], r_gain.at[j - 1], dev(x + j, y, z, core))

    def m_gy(j):
        ref = gy.at[y]
        return copy(ref, ref, s_gain.at[2 + j], r_gain.at[2 + j], dev(x, y + j, z, core))

    def m_gz(d, s):
        sg = 1 - 2 * d
        ref = gz.at[rem(z - sg * s, NZ)]
        at = 6 + d * 4 + s
        return copy(ref, ref, s_gain.at[at], r_gain.at[at], dev(x, y, z + sg, core))

    def m_gs():
        return copy(gfin.at[core], gfin.at[core], s_gain.at[14], r_gain.at[14], sib)

    partner = x + 1 - 2 * xl
    fins = (dev(partner, y, z, core), sib, dev(partner, y, z, other))

    def m_fin(i, part):
        ref = fin.at[xl, core, pl.ds((0, HGA, HGA + HGB)[part], (HGA, HGB, HGC)[part])]
        return copy(ref, ref, s_fin.at[i * 3 + part], r_fin.at[i * 3 + part], fins[i])

    def share(part):
        for i in range(3):
            m_fin(i, part).start()

    loop(4, lambda p: c_tok(p).start())
    c_kg().start()

    barrier = pltpu.get_barrier_semaphore()

    def signal(device):
        pl.semaphore_signal(barrier, inc=1, device_id=device, device_id_type=MESH)

    loop(NX, lambda j: signal(dev(x + j, y, z, core)), 1)
    loop(NY, lambda j: signal(dev(x, y + j, z, core)), 1)
    for hops in (1, 2):
        signal(dev(x, y, z + hops, core))
        signal(dev(x, y, z - hops, core))
    signal(sib)
    signal(fins[2])

    scale_t = scales[...].T
    for b in range(4):
        scale = jnp.where(core == 0, scale_t[:, b : b + 1], scale_t[:, 4 + b : 5 + b])
        code = codes[:, pl.ds(pl.multiple_of(core * HALF + b * BLOCK, BLOCK), BLOCK)]
        stage[:, column(b)] = (code.astype(F32) * scale).astype(BF16)
    for first, last, row, block in SEG_A:
        wa[z, 0, 0, first:last] = stage[row : row + last - first, column(block)]
    for mine in range(2):

        @pl.when(xl == mine)
        def _():
            for first, last, row, block in SEG_B:
                if first // HB == mine:
                    wb[y, z, 0, first - mine * HB : last - mine * HB] = stage[row : row + last - first, column(block)]
            for first, last, row, block in SEG_C:
                if first // HC == mine:
                    wc[x, z, 0, first - mine * HC : last - mine * HC] = stage[row : row + last - first, column(block)]

    pl.semaphore_wait(barrier, 12)
    m_ax().start()
    for j in range(1, NY):
        m_ay(0, j).start()
    for part in (1, 0):
        for hops in (2, 1):
            for d in range(2):
                m_z(part, d, hops, 0).start()
    d_kg().start()
    loop(4, lambda k: d_tok(pair(k)).start())
    acc[...] = jnp.zeros_like(acc)
    loop(4, lambda p: c_tok(p).wait())
    c_kg().wait()
    d_kg().wait_recv()

    def consume(k):
        p = pair(k)

        def rows_of(i):
            zz, yy, hh = 2 * p + i // 8, lax.rem(i // 2, 4), lax.rem(i, 2)
            base = zz * SLAB + yy * 160 + hh * ROWS
            for first, last, row, block in SEG_A:
                wf[pl.ds(pl.multiple_of(base + row, 16), last - first), column(block)] = wa[
                    zz, (hh + xh) % 2, rem(yy - y, NY), first:last
                ]
            for first, last, row, block in SEG_B:
                at = first // HB
                wf[pl.ds(pl.multiple_of(base + row, 16), last - first), column(block)] = wb[
                    yy, zz, rem(2 * hh + at - x, NX), first - at * HB : last - at * HB
                ]
            for first, last, row, block in SEG_C:
                at = first // HC
                wf[pl.ds(pl.multiple_of(base + row, 16), last - first), column(block)] = wc[
                    2 * hh + at, zz, rem(yy - y, NY), first - at * HC : last - at * HC
                ]

        loop(16, rows_of)
        begin = pl.multiple_of(p * PAIR, BLOCK)
        acc[...] += jnp.dot(tokv[:, pl.ds(begin, PAIR)], wf[pl.ds(begin, PAIR), :], preferred_element_type=F32)

    def transpose(k):
        d_tok(pair(k)).wait_recv()

        def part(i):
            begin = pl.multiple_of(pair(k) * PAIR + i * 256, BLOCK)
            tokt[pl.ds(begin, 256), :] = tokv[:, pl.ds(begin, 256)].T

        loop(5, part)

    def own_columns(part, ks):
        for k in ks:
            for d in range(2):
                (m_cx if part else m_by)(k, 0, d, 0).start()
            for j in range(1, 4):
                (m_cy if part else m_bx)(k, j).start()

    def far_z(part, wait):
        for d, begin in ((0, 1), (1, 1), (1 - part, 2)):
            move = m_z(part, d, 2, begin)
            move.wait_recv() if wait else move.start()

    def columns(k):
        for j in range(1, NY):
            m_cy(k, j).wait_recv()
        for d in range(2):
            m_cx(k, 1, d, 0).start()
        for j in range(1, NX):
            m_bx(k, j).wait_recv()
        for d in range(2):
            m_by(k, 1, d, 0).start()

    def own_forward(k):
        for d in range(2):
            m_cx(k, 0, d, 0).wait_recv()
            m_cx(k, 0, d, 1).start()
            m_by(k, 0, d, 0).wait_recv()
            m_by(k, 0, d, 1).start()

    m_ax().wait_recv()
    for j in range(1, NY):
        m_ay(1, j).start()
    for part in (1, 0):
        for hops in (1, 2):
            for d in range(2):
                m_z(part, d, hops, 0).wait_recv()
        far_z(part, False)
        own_columns(part, (0, 1))
    for j in range(1, NY):
        m_ay(0, j).wait_recv()
    for u in (0, 1):
        for d in range(2):
            m_az(d, 0, u).start()
    far_z(1, True)
    own_columns(1, (2, 3))
    far_z(0, True)
    own_columns(0, (2, 3))
    for j in range(1, NY):
        m_ay(1, j).wait_recv()
    for u in (2, 3):
        for d in range(2):
            m_az(d, 0, u).start()
    for u in (0, 1):
        for d in range(2):
            m_az(d, 0, u).wait_recv()
            m_az(d, 1, u).start()
    loop(2, columns)
    loop(2, own_forward)
    for u in (2, 3):
        for d in range(2):
            m_az(d, 0, u).wait_recv()
            m_az(d, 1, u).start()

    def forward(k):
        for d in range(2):
            m_cx(k, 1, d, 0).wait_recv()
            m_cx(k, 1, d, 1).start()
            m_by(k, 1, d, 0).wait_recv()
            m_by(k, 1, d, 1).start()

    def later(k):
        columns(k)
        forward(k - 2)
        own_forward(k)

    loop(4, later, 2)

    def ring(k):
        for u in range(4):
            for d in range(2):

                @pl.when(k < 2 + (u % 2 == d))
                def _():
                    m_az(d, k + 1, u).wait_recv()

                @pl.when(k < 1 + (u % 2 == d))
                def _():
                    m_az(d, k + 2, u).start()

        @pl.when(k < 2)
        def _():
            forward(k + 2)

        @pl.when(k < 4)
        def _():
            transpose(k)

        @pl.when(k > 0)
        def _():
            last_hops(k - 1)
            consume(k - 1)

    def last_hops(k):
        for unit in range(2):
            for d in range(2):
                m_cx(k, unit, d, 1).wait_recv()
                m_by(k, unit, d, 1).wait_recv()

    loop(5, ring)

    gains = gain[0:1, pl.ds(pl.multiple_of(core * HALF, BLOCK), HALF)]
    lane = lax.broadcasted_iota(jnp.int32, (8, BLOCK), 1)
    CH = 64

    def sums(i, packed):
        rows = pl.ds(pl.multiple_of(i * CH, CH), CH)
        k_raw = acc[rows, :]
        dn = kgv[rows, :].astype(F32) * gains
        one = jnp.sum(k_raw * k_raw, axis=1, keepdims=True)
        two = jnp.sum(dn * k_raw, axis=1, keepdims=True)
        for j in range(CH // 8):
            here = lane == i * (CH // 8) + j
            packed = (
                jnp.where(here, one[8 * j : 8 * j + 8], packed[0]),
                jnp.where(here, two[8 * j : 8 * j + 8], packed[1]),
            )
        return packed

    nothing = jnp.zeros((8, BLOCK), F32)
    stats[0, 0], stats[0, 1] = lax.fori_loop(0, 2 * T // CH, sums, (nothing, nothing))
    d_stats().start()
    d_stats().wait_recv()
    stats[2] = (stats[0] + stats[1]) * (1.0 / W)
    gx[x] = jnp.zeros((8, HALF), F32)

    def factors(i):
        rinvs, means = [], []
        for j in range(CH // 8):
            here = lane == i * (CH // 8) + j
            rinv = lax.rsqrt(jnp.sum(jnp.where(here, stats[2, 0], 0.0), axis=1, keepdims=True) + EPS)
            rinvs.append(rinv)
            means.append(rinv * jnp.sum(jnp.where(here, stats[2, 1], 0.0), axis=1, keepdims=True))
        return jnp.concatenate(rinvs, axis=0), jnp.concatenate(means, axis=0)

    def norm(i):
        rows = pl.ds(pl.multiple_of(i * CH, CH), CH)
        rinv, mean = factors(i)
        draw[rows, :] = (rinv * (kgv[rows, :].astype(F32) * gains - acc[rows, :] * (rinv * mean))).astype(BF16)

    loop(2 * T // CH, norm)

    def norm_keys(i):
        rows = pl.ds(pl.multiple_of(i * CH, CH), CH)
        normed = acc[rows, :] * factors(i)[0]
        keyv[rows, :] = (normed * gains).astype(BF16)
        gx[x] += jnp.sum((kgv[rows, :].astype(F32) * normed).reshape(CH // 8, 8, HALF), axis=0)

    def grad(t):
        k = t // 2
        e = rem(z + t, 2)
        zz = 2 * pair(3 - k) + e
        begin = pl.multiple_of(zz * SLAB, BLOCK)
        part = jnp.dot(tokt[pl.ds(begin, SLAB), :], draw[...], preferred_element_type=F32).astype(BF16)
        for yy in range(NY):
            for hh in range(2):
                base = yy * 160 + hh * ROWS
                for first, last, row, block in SEG_GA:
                    value = part[base + row : base + row + last - first, block * BLOCK : (block + 1) * BLOCK]
                    ga[zz, rem(yy - y, NY), hh, first:last] = value
                for first, last, row, block in SEG_GB:
                    value = part[base + row : base + row + last - first, block * BLOCK : (block + 1) * BLOCK]
                    at = first // HGB
                    gb[yy, zz, hh, at, first - at * HGB : last - at * HGB] = value
                for first, last, row, block in SEG_GC:
                    value = part[base + row : base + row + last - first, block * BLOCK : (block + 1) * BLOCK]
                    at = first // HGC
                    gc[2 * hh + at, zz, yy, first - at * HGC : last - at * HGC] = value

        m_rc(k, e, 0).start()
        m_rb(k, e, 0).start()

        @pl.when(t == 0)
        def _():
            for u in UNITS:
                m_a(u % 2 ^ 1, u, 0, True).start()

        for at, d in ((1, 1 - lax.rem(z, 2)), (3, lax.rem(z, 2))):

            @pl.when(t == at)
            def _():
                for i in range(2):
                    m_a(d, d + 2 * i, 1, True).start()

    def finish(k):
        q = pair(3 - k)
        for d in range(2):
            m_rc(k, d, 1).wait_recv()
            m_rc(k, d, 2).wait_recv()
        for h in range(2):
            ref = gc.at[x, 2 * q + h]
            ref[...] += rc[k, h, 2] + rc[k, 1 - h, 1]
        loop(NY, lambda j: m_rcy(k, j).start(), 1)
        for d in range(2):
            m_rb(k, d, 1).wait_recv()
            m_rb(k, d, 2).wait_recv()
        for h in range(2):
            ref = gb.at[y, 2 * q + h]
            ref[...] += rb[k, h, 2] + rb[k, 1 - h, 1]
        loop(NX, lambda j: m_rbx(k, j).start(), 1)

    def short(k):
        for j in range(1, NY):
            m_rcy(k, j).wait_recv()
            m_rbx(k, j).wait_recv()

        def slab(i):
            zz = 2 * pair(3 - k) + i
            ref = gc.at[x, zz, y]
            ref[...] = add(ref, *(rcy.at[i, zz] for i in range(3))).astype(BF16)
            ref = gb.at[y, zz, xh, xl]
            ref[...] = add(ref, *(rbx.at[i, zz] for i in range(3))).astype(BF16)

        loop(2, slab)
        for part, d in ((1, 0), (1, 1), (0, 0), (0, 1)):
            begin = 0 if part != d else 1
            to = rem(z + (1 - 2 * d) * (4 - k), NZ)

            @pl.when(k == begin)
            def _():
                m_rz(part, d, begin, True).start()

            @pl.when(k > begin)
            def _():
                m_rz(part, d, k - 1, True).wait_recv()
                if part:
                    rcz[d, k - 1] += gc[x, to, y]
                else:
                    rbz[d, k - 1] += gb[y, to, xh, xl]
                m_rz(part, d, k).start()

    def token_part(p):
        begin = pl.multiple_of(p * PAIR, BLOCK)
        weight = wf[pl.ds(begin, PAIR), :]
        for to in (other, core):
            rows = pl.ds(pl.multiple_of(to * T, T), T)
            tokv[rows, pl.ds(begin, PAIR)] = lax.dot_general(
                draw[rows, :], weight, (((1,), (1,)), ((), ())), preferred_element_type=F32
            ).astype(BF16)
        d_tg(p).start()

    def gain_step(s):
        for d in range(2):
            m_gz(d, s).wait_recv()
            m_gz(d, s + 1).start()

    def reduce(k):
        for d in range(2):
            sg = 1 - 2 * d
            q = pair(3 - k)
            m_rc(k, d, 0).wait_recv()
            ref = rc.at[k, d, 0]
            ref[...] += gc[rem(x + sg, NX), 2 * q + d]
            m_rc(k, d, 2).start()
            m_rb(k, d, 0).wait_recv()
            ref = rb.at[k, d, 0]
            ref[...] += gb[rem(y + sg, NY), 2 * q + d]
            m_rb(k, d, 2).start()
        for d in range(2):
            m_rc(k, d, 1).start()
            m_rb(k, d, 1).start()

        for u in UNITS:
            for d in range(2):
                sg = 1 - 2 * d

                @pl.when((k < 3) & (k >= (0 if far(d, u) else 1)))
                def _():
                    m_a(d, u, k, True).wait_recv()
                    raa[d, u, k] += ga[rem(z + sg * (3 - k), NZ), u]
                    m_a(d, u, k + 1).start()

        @pl.when(k > 0)
        def _():
            finish(k - 1)

        @pl.when(k > 1)
        def _():
            short(k - 2)

        @pl.when(k == 1)
        def _():
            loop(NX, lambda j: m_gx(j).wait_recv(), 1)
            gy[y] = add(*(gx.at[i] for i in range(NX)))
            loop(NY, lambda j: m_gy(j).start(), 1)

        @pl.when(k == 2)
        def _():
            loop(NY, lambda j: m_gy(j).wait_recv(), 1)
            gz[z] = add(*(gy.at[i] for i in range(NY)))
            for d in range(2):
                m_gz(d, 0).start()

        @pl.when(k == 3)
        def _():
            gain_step(0)

        loop(k + k // 3, token_part, k - (k + 3) // 4)

    def step(t):
        @pl.when((t < 6) | (t == 7) | (t == 8))
        def _():
            grad(t - t // 7)

        @pl.when(t == 9)
        def _():
            loop(2 * T // CH, norm_keys)
            d_keys().start()
            c_keys().start()
            loop(NX, lambda j: m_gx(j).start(), 1)

        @pl.when((t == 6) | (t > 8))
        def _():
            reduce((t - 6) - 2 * ((t - 6) // 3))

    loop(12, step)
    finish(3)
    gain_step(1)
    short(2)
    for u in UNITS:
        for d in range(2):
            m_a(d, u, 3, True).wait_recv()
        ref = ga.at[z, u]
        ref[...] += raa[0, u, 3] + raa[1, u, 3]
        if u > 0:
            m_ray(u).start()

    loop(NY, lambda j: m_ray(j).wait_recv(), 1)
    ref = ga.at[z, 0]
    ref[...] = add(ref, *(ray.at[i] for i in range(3))).astype(BF16)
    loop(NX, lambda j: m_rax(j).start(), 1)
    short(3)
    m_gz(0, 2).wait_recv()
    m_gz(1, 2).wait_recv()
    m_gz(0, 3).start()

    loop(NX, lambda j: m_rax(j).wait_recv(), 1)
    mine = fin.at[xl, core]
    own = ga.at[z, 0, xh, pl.ds(pl.multiple_of(xl * HGA, 16), HGA)]
    mine[0:HGA] = add(own, *(rax.at[i] for i in range(3))).astype(BF16)
    share(0)

    def token_sum(p):
        d_tg(p).wait()
        begin = pl.multiple_of(p * PAIR, BLOCK)
        cols = pl.ds(begin, PAIR)
        rows = pl.ds(pl.multiple_of(core * T, T), T)
        tg_out[:, cols] = (tokv[rows, cols].astype(F32) + tgr[:, cols].astype(F32)).astype(BF16)

    loop(4, token_sum)
    for d in range(2):
        m_rz(1, d, 3).wait_recv()
    mine[HGA + HGB :] = add(gc.at[x, z, y], rcz.at[0, 3], rcz.at[1, 3]).astype(BF16)
    share(2)
    for d in range(2):
        m_rz(0, d, 3).wait_recv()
    mine[HGA : HGA + HGB] = add(gb.at[y, z, xh, xl], rbz.at[0, 3], rbz.at[1, 3]).astype(BF16)
    share(1)
    m_gz(0, 3).wait_recv()
    total = add(*(gz.at[i] for i in range(NZ)))
    gfin[core] = jnp.broadcast_to(jnp.sum(total, axis=0, keepdims=True), (8, HALF))
    m_gs().start()

    m_ax().wait_send()

    def drain_y(j):
        m_ray(j).wait_send()
        m_gy(j).wait_send()

    def drain_x(j):
        m_rax(j).wait_send()
        m_gx(j).wait_send()

    loop(NY, drain_y, 1)
    loop(NX, drain_x, 1)

    def drain(k):
        def inner(j):
            m_bx(k, j).wait_send()
            m_cy(k, j).wait_send()
            m_rbx(k, j).wait_send()
            m_rcy(k, j).wait_send()

        loop(4, inner, 1)
        for d in range(2):
            for hop in range(2):
                for unit in range(2):
                    m_by(k, unit, d, hop).wait_send()
                    m_cx(k, unit, d, hop).wait_send()
            for what in range(3):
                m_rb(k, d, what).wait_send()
                m_rc(k, d, what).wait_send()
            for u in range(4):

                @pl.when(k < 3 + (u % 2 == d))
                def _():
                    m_az(d, k, u).wait_send()

            for u in range(4):

                @pl.when(k >= (0 if far(d, u) else 1))
                def _():
                    m_a(d, u, k, True).wait_send()

            @pl.when(k < 4 - d)
            def _():
                m_gz(d, k).wait_send()

            @pl.when(k >= d)
            def _():
                m_rz(1, d, k, True).wait_send()

            @pl.when(k >= 1 - d)
            def _():
                m_rz(0, d, k, True).wait_send()

        d_tok(k).wait_send()

    loop(4, drain)
    for u in range(2):
        for j in range(1, NY):
            m_ay(u, j).wait_send()
    for part in range(2):
        for d, hops, begin in ((0, 1, 0), (1, 1, 0), (0, 2, 0), (1, 2, 0), (0, 2, 1), (1, 2, 1), (1 - part, 2, 2)):
            m_z(part, d, hops, begin).wait_send()
    d_kg().wait_send()
    d_stats().wait_send()
    d_keys().wait()
    c_keys().wait()

    for i in range(3):
        for part in range(3):
            m_fin(i, part).wait()
    m_gs().wait()
    for c in range(2):
        for half in range(2):
            for segs, at, size in ((SEG_GA, 0, HGA), (SEG_GB, HGA, HGB), (SEG_GC, HGA + HGB, HGC)):
                for first, last, row, block in segs:
                    if first // size == half:
                        wg_out[row : row + last - first, column(4 * c + block)] = fin[
                            half, c, at + first - half * size : at + last - half * size
                        ].astype(F32)
        gg_out[:, c * HALF : (c + 1) * HALF] = gfin[c, 0:1]


def scratch():
    vmem, dma = pltpu.VMEM, pltpu.SemaphoreType.DMA
    both = lambda n: [dma((n,)), dma((n,))]
    buffers = [
        vmem((2 * T, D), BF16),
        vmem((D, 2 * T), BF16),
        vmem((2 * T, HALF), BF16),
        vmem((D, HALF), BF16),
        vmem((NZ, 2, NY, RA, BLOCK), BF16),
        vmem((NY, NZ, NX, HB, BLOCK), BF16),
        vmem((NX, NZ, NY, HC, BLOCK), BF16),
        vmem((2 * T, HALF), F32),
        vmem((2 * T, HALF), BF16),
        vmem((2 * T, HALF), BF16),
        vmem((3, 2, 8, BLOCK), F32),
        vmem((NZ, NY, 2, GA, BLOCK), BF16),
        vmem((NY, NZ, 2, 2, HGB, BLOCK), BF16),
        vmem((NX, NZ, NY, HGC, BLOCK), BF16),
        vmem((2, 4, 4, 2, GA, BLOCK), BF16),
        vmem((4, 2, 3, 2, 2, HGB, BLOCK), BF16),
        vmem((4, 2, 3, NY, HGC, BLOCK), BF16),
        vmem((3, 2, GA, BLOCK), BF16),
        vmem((3, HGA, BLOCK), BF16),
        vmem((3, NZ, HGB, BLOCK), BF16),
        vmem((2, 4, HGB, BLOCK), BF16),
        vmem((3, NZ, HGC, BLOCK), BF16),
        vmem((2, 4, HGC, BLOCK), BF16),
        vmem((T, D), BF16),
        vmem((NX, 8, HALF), F32),
        vmem((NY, 8, HALF), F32),
        vmem((NZ, 8, HALF), F32),
        vmem((2, 8, HALF), F32),
        vmem((2, 2, HGA + HGB + HGC, BLOCK), BF16),
        vmem((ROWS, HALF), BF16),
    ]
    semaphores = [dma((5,)), dma((5,))]
    for n in (11, 1, 6, 32, 16, 12, 12, 32, 32, 32, 48, 46, 15, 9):
        semaphores += both(n)
    return buffers + semaphores


def local(tokens, codes, scales, norm_gain, key_grad):
    hbm, vmem = pl.BlockSpec(memory_space=pl.ANY), pl.BlockSpec(memory_space=pltpu.VMEM)
    keys, token_grad, weight_grad, gain_grad = pl.pallas_call(
        kernel,
        out_shape=(
            pltpu.VMEM((T, W), BF16),
            pltpu.VMEM((T, D), BF16),
            pltpu.VMEM((ROWS, W), F32),
            pltpu.VMEM((1, W), F32),
        ),
        in_specs=[hbm, vmem, vmem, vmem, hbm],
        out_specs=(vmem, vmem, vmem, vmem),
        scratch_shapes=scratch(),
        compiler_params=pltpu.CompilerParams(collective_id=0, has_side_effects=True, vmem_limit_bytes=58 << 20),
        cost_estimate=pl.CostEstimate(flops=6 * T * D * W, bytes_accessed=12 << 20, transcendentals=0),
    )(tokens, codes, scales.T, norm_gain.reshape(1, W), key_grad)
    return keys, token_grad, weight_grad, gain_grad.reshape(W)


def solution(mesh):
    return jax.shard_map(
        local,
        mesh=mesh,
        in_specs=(P(("dp", "fsdp"), None), P("fsdp", None), P("fsdp", None), P(), P(("dp", "fsdp"), None)),
        out_specs=(P(("dp", "fsdp"), None), P(("dp", "fsdp"), None), P("fsdp", None), P()),
        check_vma=False,
    )
```

```python
import jax
import jax.numpy as jnp
from jax import lax
from jax.experimental import pallas as pl
from jax.experimental.pallas import tpu as pltpu
from jax.sharding import PartitionSpec as P

MESH = pl.DeviceIdType.MESH
F32, BF16 = jnp.float32, jnp.bfloat16
BLOCK = 128
EPS = 1e-06
D, W, T, ROWS = 5120, 1024, 384, 80
HALF = W // 2
SLAB = 640
PAIR = 2 * SLAB
RA, RB, RC = 96, 128, 96
GA, GB, GC = 96, 128, 96
NX, NY, NZ = 4, 4, 8
UNITS = (1, 2, 3, 0)


def segments(rows, block, offset, half):
    cuts = []
    for first, last, row, column in ((0, ROWS, 0, block), (ROWS, rows, offset, 3)):
        if first < half < last:
            cuts += [(first, half, row, column), (half, last, row + half - first, column)]
        else:
            cuts.append((first, last, row, column))
    return cuts


def parts(a, b, c):
    return (
        (segments(a, 0, 0, a // 2), a // 2),
        (segments(b, 1, a - ROWS, b // 2), b // 2),
        (segments(c, 2, a + b - 2 * ROWS, c // 2), c // 2),
    )


(SEG_A, HA), (SEG_B, HB), (SEG_C, HC) = parts(RA, RB, RC)
(SEG_GA, HGA), (SEG_GB, HGB), (SEG_GC, HGC) = parts(GA, GB, GC)


def column(block):
    return pl.ds(block * BLOCK, BLOCK)


def rem(a, n):
    return lax.rem(a + 2 * n, n)


def add(*refs):
    total = refs[0][...].astype(F32)
    for ref in refs[1:]:
        total = total + ref[...].astype(F32)
    return total


def kernel(
    tokens, codes, scales, gain, key_grad,
    keys_out, tg_out, wg_out, gg_out,
    tokv, tokt, kgv, wf, wa, wb, wc, acc, draw, keyv, stats,
    ga, gb, gc, raa, rb, rc, ray, rax, rbx, rbz, rcy, rcz, tgr, gx, gy, gz, gfin, fin, stage,
    s_loc, s_out,
    s_d2d, r_d2d, s_ax, r_ax, s_ay, r_ay, s_az, r_az, s_z, r_z, s_bx, r_bx, s_cy, r_cy, s_by, r_by, s_cx, r_cx,
    s_raa, r_raa, s_rr, r_rr, s_one, r_one, s_gain, r_gain, s_fin, r_fin,
):
    dp, fs = lax.axis_index("dp"), lax.axis_index("fsdp")
    xl, core = dp // 2, lax.rem(dp, 2)
    z, y, xh = fs // 8, lax.rem(fs // 2, 4), lax.rem(fs, 2)
    x = xh * 2 + xl
    other = 1 - core
    sign = 2 * lax.rem(z, 2) - 1

    def dev(x_, y_, z_, c_):
        x_, y_, z_ = rem(x_, NX), rem(y_, NY), rem(z_, NZ)
        return (lax.rem(x_, 2) * 2 + c_, z_ * 8 + y_ * 2 + x_ // 2)

    def copy(src, dst, send, recv, device):
        return pltpu.make_async_remote_copy(
            src_ref=src, dst_ref=dst, send_sem=send, recv_sem=recv, device_id=device, device_id_type=MESH
        )

    def pair(k):
        return rem(z // 2 + sign * (k + k // 2 - 2 * (k // 3)), 4)

    def loop(n, body, first=0):
        lax.fori_loop(first, n, lambda i, c: (body(i), c)[1], 0)

    sib = dev(x, y, z, other)

    def c_tok(p):
        cols = pl.ds(p * PAIR, PAIR)
        return pltpu.make_async_copy(tokens.at[:, cols], tokv.at[pl.ds(core * T, T), cols], s_loc.at[p])

    def d_tok(p):
        cols = pl.ds(p * PAIR, PAIR)
        return copy(tokens.at[:, cols], tokv.at[pl.ds(core * T, T), cols], s_d2d.at[p], r_d2d.at[p], sib)

    def c_kg():
        return pltpu.make_async_copy(
            key_grad.at[:, pl.ds(core * HALF, HALF)], kgv.at[pl.ds(core * T, T)], s_loc.at[4]
        )

    def d_kg():
        return copy(
            key_grad.at[:, pl.ds(other * HALF, HALF)], kgv.at[pl.ds(core * T, T)], s_d2d.at[4], r_d2d.at[4], sib
        )

    def d_stats():
        return copy(stats.at[0], stats.at[1], s_d2d.at[5], r_d2d.at[5], sib)

    def d_keys():
        return copy(
            keyv.at[pl.ds(other * T, T)], keys_out.at[:, pl.ds(core * HALF, HALF)], s_d2d.at[6], r_d2d.at[6], sib
        )

    def c_keys():
        return pltpu.make_async_copy(
            keyv.at[pl.ds(core * T, T)], keys_out.at[:, pl.ds(core * HALF, HALF)], s_out.at[4]
        )

    def d_tg(p):
        cols = pl.ds(p * PAIR, PAIR)
        return copy(tokv.at[pl.ds(other * T, T), cols], tgr.at[:, cols], s_d2d.at[7 + p], r_d2d.at[7 + p], sib)

    def m_ax():
        return copy(wa.at[z, 0, 0], wa.at[z, 1, 0], s_ax.at[0], r_ax.at[0], dev(3 - x, y, z, core))

    def m_ay(u, j):
        at = u * 3 + j - 1
        return copy(wa.at[z, u, 0], wa.at[z, u, 4 - j], s_ay.at[at], r_ay.at[at], dev(x, y + j, z, core))

    def m_az(d, s, u):
        sg = 1 - 2 * d
        ref = wa.at[rem(z - sg * s, NZ), u // 2, pl.ds(2 * (u % 2), 2)]
        at = (s * 4 + u) * 2 + d
        return copy(ref, ref, s_az.at[at], r_az.at[at], dev(x, y, z + sg, core))

    def m_z(part, d, hops, begin):
        sg = 1 - 2 * d
        to = rem(z - sg * begin, NZ)
        ref = wc.at[x, to, 0] if part else wb.at[y, to, 0]
        at = ((part * 2 + d) * 2 + (begin > 0)) * 2 + (begin or hops) - 1
        return copy(ref, ref, s_z.at[at], r_z.at[at], dev(x, y, z + sg * hops, core))

    def m_bx(k, j):
        zs = pl.ds(2 * pair(k), 2)
        at = k * 3 + j - 1
        return copy(wb.at[y, zs, 0], wb.at[y, zs, 4 - j], s_bx.at[at], r_bx.at[at], dev(x + j, y, z, core))

    def m_cy(k, j):
        zs = pl.ds(2 * pair(k), 2)
        at = k * 3 + j - 1
        return copy(wc.at[x, zs, 0], wc.at[x, zs, 4 - j], s_cy.at[at], r_cy.at[at], dev(x, y + j, z, core))

    def long_ring(buf, me, k, unit, d, hop):
        slots = pl.ds(1, 3) if unit else pl.ds(0, 1)
        if hop == 0:
            return buf.at[me, pl.ds(2 * pair(k), 2), slots]
        return buf.at[rem(me - 1 + 2 * d, 4), 2 * pair(k) + d, slots]

    def m_by(k, unit, d, hop):
        ref = long_ring(wb, y, k, unit, d, hop)
        at = ((k * 2 + unit) * 2 + hop) * 2 + d
        return copy(ref, ref, s_by.at[at], r_by.at[at], dev(x, y + 1 - 2 * d, z, core))

    def m_cx(k, unit, d, hop):
        ref = long_ring(wc, x, k, unit, d, hop)
        at = ((k * 2 + unit) * 2 + hop) * 2 + d
        return copy(ref, ref, s_cx.at[at], r_cx.at[at], dev(x + 1 - 2 * d, y, z, core))

    def far(d, u):
        return u % 2 == 1 - d

    def m_a(d, u, s, first=False):
        sg = 1 - 2 * d
        src = ga.at[rem(z + sg * (4 - s), NZ), u] if first else raa.at[d, u, s - 1]
        at = (d * 4 + u) * 4 + s
        return copy(src, raa.at[d, u, s], s_raa.at[at], r_raa.at[at], dev(x, y, z + sg, core))

    def m_rb(k, d, what):
        sg = 1 - 2 * d
        q = pair(3 - k)
        src = (
            gb.at[rem(y + 2, NY), 2 * q + d],
            gb.at[rem(y + sg, NY), 2 * q + 1 - d],
            rb.at[k, d, 0],
        )[what]
        at = (k * 2 + d) * 3 + what
        return copy(src, rb.at[k, d, what], s_rr.at[at], r_rr.at[at], dev(x, y + sg, z, core))

    def m_rc(k, d, what):
        sg = 1 - 2 * d
        q = pair(3 - k)
        src = (
            gc.at[rem(x + 2, NX), 2 * q + d],
            gc.at[rem(x + sg, NX), 2 * q + 1 - d],
            rc.at[k, d, 0],
        )[what]
        at = 24 + (k * 2 + d) * 3 + what
        return copy(src, rc.at[k, d, what], s_rr.at[at], r_rr.at[at], dev(x + sg, y, z, core))

    def m_rbx(k, j):
        to = rem(x + j, NX)
        zs = pl.ds(2 * pair(3 - k), 2)
        at = k * 3 + j - 1
        return copy(
            gb.at[y, zs, to // 2, lax.rem(to, 2)], rbx.at[j - 1, zs], s_one.at[at], r_one.at[at], dev(to, y, z, core)
        )

    def m_rcy(k, j):
        to = rem(y + j, NY)
        zs = pl.ds(2 * pair(3 - k), 2)
        at = 12 + k * 3 + j - 1
        return copy(gc.at[x, zs, to], rcy.at[j - 1, zs], s_one.at[at], r_one.at[at], dev(x, to, z, core))

    def m_rz(part, d, s, first=False):
        sg = 1 - 2 * d
        to = rem(z + sg * (4 - s), NZ)
        own, held = (gc.at[x, to, y], rcz) if part else (gb.at[y, to, xh, xl], rbz)
        at = 24 + (part * 2 + d) * 4 + s
        return copy(own if first else held.at[d, s - 1], held.at[d, s], s_one.at[at], r_one.at[at], dev(x, y, z + sg, core))

    def m_ray(j):
        to = rem(y + j, NY)
        at = 39 + j
        return copy(ga.at[z, j], ray.at[j - 1], s_one.at[at], r_one.at[at], dev(x, to, z, core))

    def m_rax(j):
        to = rem(x + j, NX)
        at = 42 + j
        src = ga.at[z, 0, to // 2, pl.ds(lax.rem(to, 2) * HGA, HGA)]
        return copy(src, rax.at[j - 1], s_one.at[at], r_one.at[at], dev(to, y, z, core))

    def m_gx(j):
        ref = gx.at[x]
        return copy(ref, ref, s_gain.at[j - 1], r_gain.at[j - 1], dev(x + j, y, z, core))

    def m_gy(j):
        ref = gy.at[y]
        return copy(ref, ref, s_gain.at[2 + j], r_gain.at[2 + j], dev(x, y + j, z, core))

    def m_gz(d, s):
        sg = 1 - 2 * d
        ref = gz.at[rem(z - sg * s, NZ)]
        at = 6 + d * 4 + s
        return copy(ref, ref, s_gain.at[at], r_gain.at[at], dev(x, y, z + sg, core))

    def m_gs():
        return copy(gfin.at[core], gfin.at[core], s_gain.at[14], r_gain.at[14], sib)

    partner = x + 1 - 2 * xl
    fins = (dev(partner, y, z, core), sib, dev(partner, y, z, other))

    def m_fin(i, part):
        ref = fin.at[xl, core, pl.ds((0, HGA, HGA + HGB)[part], (HGA, HGB, HGC)[part])]
        return copy(ref, ref, s_fin.at[i * 3 + part], r_fin.at[i * 3 + part], fins[i])

    def share(part):
        for i in range(3):
            m_fin(i, part).start()

    barrier = pltpu.get_barrier_semaphore()

    def signal(device):
        pl.semaphore_signal(barrier, inc=1, device_id=device, device_id_type=MESH)

    loop(NX, lambda j: signal(dev(x + j, y, z, core)), 1)
    loop(NY, lambda j: signal(dev(x, y + j, z, core)), 1)
    for hops in (1, 2):
        signal(dev(x, y, z + hops, core))
        signal(dev(x, y, z - hops, core))
    signal(sib)
    signal(fins[2])

    scale_t = scales[...].T
    for b in range(4):
        scale = jnp.where(core == 0, scale_t[:, b : b + 1], scale_t[:, 4 + b : 5 + b])
        code = codes[:, pl.ds(pl.multiple_of(core * HALF + b * BLOCK, BLOCK), BLOCK)]
        stage[:, column(b)] = (code.astype(F32) * scale).astype(BF16)
    for first, last, row, block in SEG_A:
        wa[z, 0, 0, first:last] = stage[row : row + last - first, column(block)]
    for mine in range(2):

        @pl.when(xl == mine)
        def _():
            for first, last, row, block in SEG_B:
                if first // HB == mine:
                    wb[y, z, 0, first - mine * HB : last - mine * HB] = stage[row : row + last - first, column(block)]
            for first, last, row, block in SEG_C:
                if first // HC == mine:
                    wc[x, z, 0, first - mine * HC : last - mine * HC] = stage[row : row + last - first, column(block)]

    loop(4, lambda p: c_tok(p).start())
    c_kg().start()
    pl.semaphore_wait(barrier, 12)
    m_ax().start()
    for j in range(1, NY):
        m_ay(0, j).start()
    for part in (1, 0):
        for hops in (2, 1):
            for d in range(2):
                m_z(part, d, hops, 0).start()
    d_kg().start()
    loop(4, lambda k: d_tok(pair(k)).start())
    acc[...] = jnp.zeros_like(acc)
    loop(4, lambda p: c_tok(p).wait())
    c_kg().wait()
    d_kg().wait_recv()

    def consume(k):
        p = pair(k)

        def rows_of(i):
            zz, yy, hh = 2 * p + i // 8, lax.rem(i // 2, 4), lax.rem(i, 2)
            base = zz * SLAB + yy * 160 + hh * ROWS
            for first, last, row, block in SEG_A:
                wf[pl.ds(pl.multiple_of(base + row, 16), last - first), column(block)] = wa[
                    zz, (hh + xh) % 2, rem(yy - y, NY), first:last
                ]
            for first, last, row, block in SEG_B:
                at = first // HB
                wf[pl.ds(pl.multiple_of(base + row, 16), last - first), column(block)] = wb[
                    yy, zz, rem(2 * hh + at - x, NX), first - at * HB : last - at * HB
                ]
            for first, last, row, block in SEG_C:
                at = first // HC
                wf[pl.ds(pl.multiple_of(base + row, 16), last - first), column(block)] = wc[
                    2 * hh + at, zz, rem(yy - y, NY), first - at * HC : last - at * HC
                ]

        loop(16, rows_of)
        begin = pl.multiple_of(p * PAIR, BLOCK)
        acc[...] += jnp.dot(tokv[:, pl.ds(begin, PAIR)], wf[pl.ds(begin, PAIR), :], preferred_element_type=F32)

    def transpose(k):
        d_tok(pair(k)).wait_recv()

        def part(i):
            begin = pl.multiple_of(pair(k) * PAIR + i * 256, BLOCK)
            tokt[pl.ds(begin, 256), :] = tokv[:, pl.ds(begin, 256)].T

        loop(5, part)

    def own_columns(part, ks):
        for k in ks:
            for d in range(2):
                (m_cx if part else m_by)(k, 0, d, 0).start()
            for j in range(1, 4):
                (m_cy if part else m_bx)(k, j).start()

    def far_z(part, wait):
        for d, begin in ((0, 1), (1, 1), (1 - part, 2)):
            move = m_z(part, d, 2, begin)
            move.wait_recv() if wait else move.start()

    def columns(k):
        for j in range(1, NY):
            m_cy(k, j).wait_recv()
        for d in range(2):
            m_cx(k, 1, d, 0).start()
        for j in range(1, NX):
            m_bx(k, j).wait_recv()
        for d in range(2):
            m_by(k, 1, d, 0).start()

    def own_forward(k):
        for d in range(2):
            m_cx(k, 0, d, 0).wait_recv()
            m_cx(k, 0, d, 1).start()
            m_by(k, 0, d, 0).wait_recv()
            m_by(k, 0, d, 1).start()

    m_ax().wait_recv()
    for j in range(1, NY):
        m_ay(1, j).start()
    for part in (1, 0):
        for hops in (1, 2):
            for d in range(2):
                m_z(part, d, hops, 0).wait_recv()
        far_z(part, False)
        own_columns(part, (0, 1))
    for j in range(1, NY):
        m_ay(0, j).wait_recv()
    for u in (0, 1):
        for d in range(2):
            m_az(d, 0, u).start()
    far_z(1, True)
    own_columns(1, (2, 3))
    far_z(0, True)
    own_columns(0, (2, 3))
    for j in range(1, NY):
        m_ay(1, j).wait_recv()
    for u in (2, 3):
        for d in range(2):
            m_az(d, 0, u).start()
    for u in (0, 1):
        for d in range(2):
            m_az(d, 0, u).wait_recv()
            m_az(d, 1, u).start()
    loop(2, columns)
    loop(2, own_forward)
    for u in (2, 3):
        for d in range(2):
            m_az(d, 0, u).wait_recv()
            m_az(d, 1, u).start()

    def forward(k):
        for d in range(2):
            m_cx(k, 1, d, 0).wait_recv()
            m_cx(k, 1, d, 1).start()
            m_by(k, 1, d, 0).wait_recv()
            m_by(k, 1, d, 1).start()

    def later(k):
        transpose(2 * k - 4)
        columns(k)
        forward(k - 2)
        own_forward(k)
        transpose(2 * k - 3)

    loop(4, later, 2)

    def ring(k):
        for u in range(4):
            for d in range(2):

                @pl.when(k < 2 + (u % 2 == d))
                def _():
                    m_az(d, k + 1, u).wait_recv()

                @pl.when(k < 1 + (u % 2 == d))
                def _():
                    m_az(d, k + 2, u).start()

        @pl.when(k < 2)
        def _():
            forward(k + 2)

        @pl.when(k > 0)
        def _():
            last_hops(k - 1)
            consume(k - 1)

    def last_hops(k):
        for unit in range(2):
            for d in range(2):
                m_cx(k, unit, d, 1).wait_recv()
                m_by(k, unit, d, 1).wait_recv()

    loop(5, ring)

    gains = gain[0:1, pl.ds(pl.multiple_of(core * HALF, BLOCK), HALF)]
    lane = lax.broadcasted_iota(jnp.int32, (8, BLOCK), 1)
    CH = 64

    def sums(i, packed):
        rows = pl.ds(pl.multiple_of(i * CH, CH), CH)
        k_raw = acc[rows, :]
        dn = kgv[rows, :].astype(F32) * gains
        one = jnp.sum(k_raw * k_raw, axis=1, keepdims=True)
        two = jnp.sum(dn * k_raw, axis=1, keepdims=True)
        for j in range(CH // 8):
            here = lane == i * (CH // 8) + j
            packed = (
                jnp.where(here, one[8 * j : 8 * j + 8], packed[0]),
                jnp.where(here, two[8 * j : 8 * j + 8], packed[1]),
            )
        return packed

    nothing = jnp.zeros((8, BLOCK), F32)
    stats[0, 0], stats[0, 1] = lax.fori_loop(0, 2 * T // CH, sums, (nothing, nothing))
    d_stats().start()
    d_stats().wait_recv()
    stats[2] = (stats[0] + stats[1]) * (1.0 / W)
    gx[x] = jnp.zeros((8, HALF), F32)

    def factors(i):
        rinvs, means = [], []
        for j in range(CH // 8):
            here = lane == i * (CH // 8) + j
            rinv = lax.rsqrt(jnp.sum(jnp.where(here, stats[2, 0], 0.0), axis=1, keepdims=True) + EPS)
            rinvs.append(rinv)
            means.append(rinv * jnp.sum(jnp.where(here, stats[2, 1], 0.0), axis=1, keepdims=True))
        return jnp.concatenate(rinvs, axis=0), jnp.concatenate(means, axis=0)

    def norm(i):
        rows = pl.ds(pl.multiple_of(i * CH, CH), CH)
        rinv, mean = factors(i)
        draw[rows, :] = (rinv * (kgv[rows, :].astype(F32) * gains - acc[rows, :] * (rinv * mean))).astype(BF16)

    loop(2 * T // CH, norm)

    def norm_keys(i):
        rows = pl.ds(pl.multiple_of(i * CH, CH), CH)
        normed = acc[rows, :] * factors(i)[0]
        keyv[rows, :] = (normed * gains).astype(BF16)
        gx[x] += jnp.sum((kgv[rows, :].astype(F32) * normed).reshape(CH // 8, 8, HALF), axis=0)

    def grad(t):
        k = t // 2
        e = rem(z + t, 2)
        zz = 2 * pair(3 - k) + e
        begin = pl.multiple_of(zz * SLAB, BLOCK)
        part = jnp.dot(tokt[pl.ds(begin, SLAB), :], draw[...], preferred_element_type=F32).astype(BF16)
        for yy in range(NY):
            for hh in range(2):
                base = yy * 160 + hh * ROWS
                for first, last, row, block in SEG_GA:
                    value = part[base + row : base + row + last - first, block * BLOCK : (block + 1) * BLOCK]
                    ga[zz, rem(yy - y, NY), hh, first:last] = value
                for first, last, row, block in SEG_GB:
                    value = part[base + row : base + row + last - first, block * BLOCK : (block + 1) * BLOCK]
                    at = first // HGB
                    gb[yy, zz, hh, at, first - at * HGB : last - at * HGB] = value
                for first, last, row, block in SEG_GC:
                    value = part[base + row : base + row + last - first, block * BLOCK : (block + 1) * BLOCK]
                    at = first // HGC
                    gc[2 * hh + at, zz, yy, first - at * HGC : last - at * HGC] = value

        m_rc(k, e, 0).start()
        m_rb(k, e, 0).start()

        @pl.when(t == 0)
        def _():
            for u in UNITS:
                m_a(u % 2 ^ 1, u, 0, True).start()

        for at, d in ((1, 1 - lax.rem(z, 2)), (3, lax.rem(z, 2))):

            @pl.when(t == at)
            def _():
                for i in range(2):
                    m_a(d, d + 2 * i, 1, True).start()

    def finish(k):
        q = pair(3 - k)
        for d in range(2):
            m_rc(k, d, 1).wait_recv()
            m_rc(k, d, 2).wait_recv()
        for h in range(2):
            ref = gc.at[x, 2 * q + h]
            ref[...] += rc[k, h, 2] + rc[k, 1 - h, 1]
        loop(NY, lambda j: m_rcy(k, j).start(), 1)
        for d in range(2):
            m_rb(k, d, 1).wait_recv()
            m_rb(k, d, 2).wait_recv()
        for h in range(2):
            ref = gb.at[y, 2 * q + h]
            ref[...] += rb[k, h, 2] + rb[k, 1 - h, 1]
        loop(NX, lambda j: m_rbx(k, j).start(), 1)

    def short(k):
        for j in range(1, NY):
            m_rcy(k, j).wait_recv()
            m_rbx(k, j).wait_recv()

        def slab(i):
            zz = 2 * pair(3 - k) + i
            ref = gc.at[x, zz, y]
            ref[...] = add(ref, *(rcy.at[i, zz] for i in range(3))).astype(BF16)
            ref = gb.at[y, zz, xh, xl]
            ref[...] = add(ref, *(rbx.at[i, zz] for i in range(3))).astype(BF16)

        loop(2, slab)
        for part, d in ((1, 0), (1, 1), (0, 0), (0, 1)):
            begin = 0 if part != d else 1
            to = rem(z + (1 - 2 * d) * (4 - k), NZ)

            @pl.when(k == begin)
            def _():
                m_rz(part, d, begin, True).start()

            @pl.when(k > begin)
            def _():
                m_rz(part, d, k - 1, True).wait_recv()
                if part:
                    rcz[d, k - 1] += gc[x, to, y]
                else:
                    rbz[d, k - 1] += gb[y, to, xh, xl]
                m_rz(part, d, k).start()

    def token_part(p):
        begin = pl.multiple_of(p * PAIR, BLOCK)
        weight = wf[pl.ds(begin, PAIR), :]
        for to in (other, core):
            rows = pl.ds(pl.multiple_of(to * T, T), T)
            tokv[rows, pl.ds(begin, PAIR)] = lax.dot_general(
                draw[rows, :], weight, (((1,), (1,)), ((), ())), preferred_element_type=F32
            ).astype(BF16)
        d_tg(p).start()

    def gain_step(s):
        for d in range(2):
            m_gz(d, s).wait_recv()
            m_gz(d, s + 1).start()

    def reduce(k):
        for d in range(2):
            sg = 1 - 2 * d
            q = pair(3 - k)
            m_rc(k, d, 0).wait_recv()
            ref = rc.at[k, d, 0]
            ref[...] += gc[rem(x + sg, NX), 2 * q + d]
            m_rc(k, d, 2).start()
            m_rb(k, d, 0).wait_recv()
            ref = rb.at[k, d, 0]
            ref[...] += gb[rem(y + sg, NY), 2 * q + d]
            m_rb(k, d, 2).start()
        for d in range(2):
            m_rc(k, d, 1).start()
            m_rb(k, d, 1).start()

        for u in UNITS:
            for d in range(2):
                sg = 1 - 2 * d

                @pl.when((k < 3) & (k >= (0 if far(d, u) else 1)))
                def _():
                    m_a(d, u, k, True).wait_recv()
                    raa[d, u, k] += ga[rem(z + sg * (3 - k), NZ), u]
                    m_a(d, u, k + 1).start()

        @pl.when(k > 0)
        def _():
            finish(k - 1)

        @pl.when(k > 1)
        def _():
            short(k - 2)

        @pl.when(k == 1)
        def _():
            loop(NX, lambda j: m_gx(j).wait_recv(), 1)
            gy[y] = add(*(gx.at[i] for i in range(NX)))
            loop(NY, lambda j: m_gy(j).start(), 1)

        @pl.when(k == 2)
        def _():
            loop(NY, lambda j: m_gy(j).wait_recv(), 1)
            gz[z] = add(*(gy.at[i] for i in range(NY)))
            for d in range(2):
                m_gz(d, 0).start()

        @pl.when(k == 3)
        def _():
            gain_step(0)

        loop(k + k // 3, token_part, k - (k + 3) // 4)

    def step(t):
        @pl.when((t < 6) | (t == 7) | (t == 8))
        def _():
            grad(t - t // 7)

        @pl.when(t == 9)
        def _():
            loop(2 * T // CH, norm_keys)
            d_keys().start()
            c_keys().start()
            loop(NX, lambda j: m_gx(j).start(), 1)

        @pl.when((t == 6) | (t > 8))
        def _():
            reduce((t - 6) - 2 * ((t - 6) // 3))

    loop(12, step)
    finish(3)
    gain_step(1)
    short(2)
    for u in UNITS:
        for d in range(2):
            m_a(d, u, 3, True).wait_recv()
        ref = ga.at[z, u]
        ref[...] += raa[0, u, 3] + raa[1, u, 3]
        if u > 0:
            m_ray(u).start()

    loop(NY, lambda j: m_ray(j).wait_recv(), 1)
    ref = ga.at[z, 0]
    ref[...] = add(ref, *(ray.at[i] for i in range(3))).astype(BF16)
    loop(NX, lambda j: m_rax(j).start(), 1)
    short(3)
    m_gz(0, 2).wait_recv()
    m_gz(1, 2).wait_recv()
    m_gz(0, 3).start()

    loop(NX, lambda j: m_rax(j).wait_recv(), 1)
    mine = fin.at[xl, core]
    own = ga.at[z, 0, xh, pl.ds(pl.multiple_of(xl * HGA, 16), HGA)]
    mine[0:HGA] = add(own, *(rax.at[i] for i in range(3))).astype(BF16)
    share(0)

    def token_sum(p):
        d_tg(p).wait()
        begin = pl.multiple_of(p * PAIR, BLOCK)
        cols = pl.ds(begin, PAIR)
        rows = pl.ds(pl.multiple_of(core * T, T), T)
        tg_out[:, cols] = (tokv[rows, cols].astype(F32) + tgr[:, cols].astype(F32)).astype(BF16)

    loop(4, token_sum)
    for d in range(2):
        m_rz(1, d, 3).wait_recv()
    mine[HGA + HGB :] = add(gc.at[x, z, y], rcz.at[0, 3], rcz.at[1, 3]).astype(BF16)
    share(2)
    for d in range(2):
        m_rz(0, d, 3).wait_recv()
    mine[HGA : HGA + HGB] = add(gb.at[y, z, xh, xl], rbz.at[0, 3], rbz.at[1, 3]).astype(BF16)
    share(1)
    m_gz(0, 3).wait_recv()
    total = add(*(gz.at[i] for i in range(NZ)))
    gfin[core] = jnp.broadcast_to(jnp.sum(total, axis=0, keepdims=True), (8, HALF))
    m_gs().start()

    m_ax().wait_send()

    def drain_y(j):
        m_ray(j).wait_send()
        m_gy(j).wait_send()

    def drain_x(j):
        m_rax(j).wait_send()
        m_gx(j).wait_send()

    loop(NY, drain_y, 1)
    loop(NX, drain_x, 1)

    def drain(k):
        def inner(j):
            m_bx(k, j).wait_send()
            m_cy(k, j).wait_send()
            m_rbx(k, j).wait_send()
            m_rcy(k, j).wait_send()

        loop(4, inner, 1)
        for d in range(2):
            for hop in range(2):
                for unit in range(2):
                    m_by(k, unit, d, hop).wait_send()
                    m_cx(k, unit, d, hop).wait_send()
            for what in range(3):
                m_rb(k, d, what).wait_send()
                m_rc(k, d, what).wait_send()
            for u in range(4):

                @pl.when(k < 3 + (u % 2 == d))
                def _():
                    m_az(d, k, u).wait_send()

            for u in range(4):

                @pl.when(k >= (0 if far(d, u) else 1))
                def _():
                    m_a(d, u, k, True).wait_send()

            @pl.when(k < 4 - d)
            def _():
                m_gz(d, k).wait_send()

            @pl.when(k >= d)
            def _():
                m_rz(1, d, k, True).wait_send()

            @pl.when(k >= 1 - d)
            def _():
                m_rz(0, d, k, True).wait_send()

        d_tok(k).wait_send()

    loop(4, drain)
    for u in range(2):
        for j in range(1, NY):
            m_ay(u, j).wait_send()
    for part in range(2):
        for d, hops, begin in ((0, 1, 0), (1, 1, 0), (0, 2, 0), (1, 2, 0), (0, 2, 1), (1, 2, 1), (1 - part, 2, 2)):
            m_z(part, d, hops, begin).wait_send()
    d_kg().wait_send()
    d_stats().wait_send()
    d_keys().wait()
    c_keys().wait()

    for i in range(3):
        for part in range(3):
            m_fin(i, part).wait()
    m_gs().wait()
    for c in range(2):
        for half in range(2):
            for segs, at, size in ((SEG_GA, 0, HGA), (SEG_GB, HGA, HGB), (SEG_GC, HGA + HGB, HGC)):
                for first, last, row, block in segs:
                    if first // size == half:
                        wg_out[row : row + last - first, column(4 * c + block)] = fin[
                            half, c, at + first - half * size : at + last - half * size
                        ].astype(F32)
        gg_out[:, c * HALF : (c + 1) * HALF] = gfin[c, 0:1]


def scratch():
    vmem, dma = pltpu.VMEM, pltpu.SemaphoreType.DMA
    both = lambda n: [dma((n,)), dma((n,))]
    buffers = [
        vmem((2 * T, D), BF16),
        vmem((D, 2 * T), BF16),
        vmem((2 * T, HALF), BF16),
        vmem((D, HALF), BF16),
        vmem((NZ, 2, NY, RA, BLOCK), BF16),
        vmem((NY, NZ, NX, HB, BLOCK), BF16),
        vmem((NX, NZ, NY, HC, BLOCK), BF16),
        vmem((2 * T, HALF), F32),
        vmem((2 * T, HALF), BF16),
        vmem((2 * T, HALF), BF16),
        vmem((3, 2, 8, BLOCK), F32),
        vmem((NZ, NY, 2, GA, BLOCK), BF16),
        vmem((NY, NZ, 2, 2, HGB, BLOCK), BF16),
        vmem((NX, NZ, NY, HGC, BLOCK), BF16),
        vmem((2, 4, 4, 2, GA, BLOCK), BF16),
        vmem((4, 2, 3, 2, 2, HGB, BLOCK), BF16),
        vmem((4, 2, 3, NY, HGC, BLOCK), BF16),
        vmem((3, 2, GA, BLOCK), BF16),
        vmem((3, HGA, BLOCK), BF16),
        vmem((3, NZ, HGB, BLOCK), BF16),
        vmem((2, 4, HGB, BLOCK), BF16),
        vmem((3, NZ, HGC, BLOCK), BF16),
        vmem((2, 4, HGC, BLOCK), BF16),
        vmem((T, D), BF16),
        vmem((NX, 8, HALF), F32),
        vmem((NY, 8, HALF), F32),
        vmem((NZ, 8, HALF), F32),
        vmem((2, 8, HALF), F32),
        vmem((2, 2, HGA + HGB + HGC, BLOCK), BF16),
        vmem((ROWS, HALF), BF16),
    ]
    semaphores = [dma((5,)), dma((5,))]
    for n in (11, 1, 6, 32, 16, 12, 12, 32, 32, 32, 48, 46, 15, 9):
        semaphores += both(n)
    return buffers + semaphores


def local(tokens, codes, scales, norm_gain, key_grad):
    hbm, vmem = pl.BlockSpec(memory_space=pl.ANY), pl.BlockSpec(memory_space=pltpu.VMEM)
    keys, token_grad, weight_grad, gain_grad = pl.pallas_call(
        kernel,
        out_shape=(
            pltpu.VMEM((T, W), BF16),
            pltpu.VMEM((T, D), BF16),
            pltpu.VMEM((ROWS, W), F32),
            pltpu.VMEM((1, W), F32),
        ),
        in_specs=[hbm, vmem, vmem, vmem, hbm],
        out_specs=(vmem, vmem, vmem, vmem),
        scratch_shapes=scratch(),
        compiler_params=pltpu.CompilerParams(collective_id=0, has_side_effects=True, vmem_limit_bytes=58 << 20),
        cost_estimate=pl.CostEstimate(flops=6 * T * D * W, bytes_accessed=12 << 20, transcendentals=0),
    )(tokens, codes, scales.T, norm_gain.reshape(1, W), key_grad)
    return keys, token_grad, weight_grad, gain_grad.reshape(W)


def solution(mesh):
    return jax.shard_map(
        local,
        mesh=mesh,
        in_specs=(P(("dp", "fsdp"), None), P("fsdp", None), P("fsdp", None), P(), P(("dp", "fsdp"), None)),
        out_specs=(P(("dp", "fsdp"), None), P(("dp", "fsdp"), None), P("fsdp", None), P()),
        check_vma=False,
    )
```
